32 devices in a mesh: tok: 8 (over y, x, core), tp: 4 (over z).
Axes of the slice: x: 2, y: 2, z: 4, core: 2. Of those that a mesh axis runs over, the one named last changes fastest.
Arguments:
- hidden: bfloat16 [16384, 8192], P('tok', 'tp'), may hold values from -6 to 6
- key_value_weight: bfloat16 [8192, 2, 1024], P('tp'), may hold values from -0.09375 to 0.09375
- adapter_down_weight: bfloat16 [16, 8192, 128], P('tok', 'tp'), may hold values from -0.0625 to 0.0625
- adapter_up_weight: bfloat16 [16, 2, 64, 1024], P('tok', None, None, 'tp'), may hold values from -0.75 to 0.75
- tenant_per_block: int32 [128], P('tok'), may hold values from 0 to 15, as said below
Outputs:
- kv: bfloat16 [16384, 2, 1024], P('tok', None, 'tp')
The draws below stay inside these ranges and needn't reach their ends.
Inputs may be any that keep to these rules, and one draw needn't show every extreme that they name: `tenant_per_block`: the index of tok that holds tenant t is t // 2. The blocks of one index of tok have at most 4 tenant held by any one index, and 1 indices hold tenants of exactly 4 blocks of every index.
All inputs are finite; a program needn't handle non-finite values.
Results may differ from the reference program's by a relative error of at most 0.02.
Values may be sent and summed in bfloat16 or wider, within the bound.
No kernel may reach another device: no remote copies, remote signals or barrier semaphores. Data moves between devices by JAX's collectives and lax.ppermute only.
A program may use at most 128 MiB of HBM per device.

```python
import jax
import jax.numpy as jnp
from jax import lax

MODEL_WIDTH = 8192
ADAPTER_RANK = 64
BLOCK = 128
TEN_DEV = 2
BLK_DEV = 16
KEY_VALUE_WIDTH = 1024
TENANT_COUNT = 16
TOKENS = 16384
NBLK = 128
CAP = 4
NHOT = 1
N_TOK = 8
N_TP = 4


def draw_tenant_per_block(key, part):
    key = jax.random.fold_in(key, 7)
    random_keys = jax.random.split(key, 4)
    tenant_slots = N_TOK * CAP
    order = jax.random.permutation(random_keys[0], N_TOK)
    frequent_tenants = order < NHOT
    tenant_owner = jnp.arange(tenant_slots) // CAP
    extra_term = jnp.where(frequent_tenants[tenant_owner], 2 ** 21, 0).astype(jnp.int32)
    tenant_score = jax.random.randint(random_keys[1], (N_TOK, tenant_slots), 0, 2 ** 20) + extra_term[None, :]
    tenant_score = tenant_score * tenant_slots + jnp.arange(tenant_slots, dtype=jnp.int32)[None, :]
    top_scores, picked = lax.top_k(tenant_score, BLK_DEV)
    shuffle = jax.random.randint(random_keys[2], (N_TOK, BLK_DEV), 0, 2 ** 20) * BLK_DEV + jnp.arange(BLK_DEV, dtype=jnp.int32)[None, :]
    position = jnp.argsort(shuffle, axis=1, stable=True)
    picked = jnp.take_along_axis(picked, position, axis=1)
    within = jax.random.randint(random_keys[3], (N_TOK, BLK_DEV), 0, TEN_DEV)
    return (picked // CAP * TEN_DEV + within).reshape(-1).astype(jnp.int32)


def spiked(result, stream_key, source, target, parts, factor):
    owner, partner = [(jnp.arange(result.shape[axis_at]) // (result.shape[axis_at] // parts)).reshape([-1 if axis == axis_at else 1 for axis in range(result.ndim)]) for axis_at in (source, target)]
    chosen = jax.random.permutation(stream_key, parts)[partner]
    strong = (owner == chosen) | (owner == (partner + parts // 2) % parts)
    return jnp.where(strong, factor * result, result)


def levels(own_key, shape, cuts, least, largest):
    loudness = 1.0
    for axis_at, blocks in cuts:
        heights = jax.random.uniform(jax.random.fold_in(jax.random.fold_in(own_key, 6), axis_at), (blocks,), jnp.float32, least / len(cuts), largest / len(cuts))
        loudness = loudness * jnp.repeat(jnp.exp(heights), shape[axis_at] // blocks).reshape((-1,) + (1,) * (len(shape) - 1 - axis_at))
    return loudness


def bell_draw(stream_key, extent, scale, bound, cuts=(), held_as=jnp.bfloat16):
    drawn = jax.random.normal(stream_key, extent, jnp.float32) * scale
    if len(cuts) > 0:
        drawn = levels(stream_key, extent, cuts, -0.22, 0.18) * drawn
    return jnp.clip(drawn, min=-bound, max=bound).astype(held_as)


def heavy_noise(rng, extent, scale, most, pieces, heavy, kind=jnp.bfloat16):
    entries = scale * jax.random.normal(rng, extent, jnp.float32)
    if pieces:
        entries = entries * levels(rng, extent, pieces, -0.22, 0.18)
    return jnp.clip(spiked(entries, jax.random.fold_in(rng, 3), *heavy), -most, most).astype(kind)


def setup_inputs(seed: int = 0) -> dict:
    key_list = jax.random.split(jax.random.key(seed), 6)
    return {
        "hidden": bell_draw(key_list[0], (TOKENS, MODEL_WIDTH), 1.0, 6.0, ((0, 8), (1, 4))),
        "key_value_weight": heavy_noise(key_list[1], (MODEL_WIDTH, 2, KEY_VALUE_WIDTH), MODEL_WIDTH ** -0.5, 0.09375, ((0, 4),), (0, 2, 4, 2.0)),
        "adapter_down_weight": bell_draw(key_list[2], (TENANT_COUNT, MODEL_WIDTH, 2 * ADAPTER_RANK), MODEL_WIDTH ** -0.5, 0.0625, ((0, 8), (1, 4))),
        "adapter_up_weight": bell_draw(key_list[3], (TENANT_COUNT, 2, ADAPTER_RANK, KEY_VALUE_WIDTH), ADAPTER_RANK ** -0.5, 0.75, ((0, 8), (3, 4))),
        "tenant_per_block": draw_tenant_per_block(jax.random.fold_in(key_list[5], 71), 0),
    }


def adapt_token_block(adapter_down_weight, adapter_up_weight, block_number, tenant_index):
    down_weight = lax.dynamic_index_in_dim(adapter_down_weight, tenant_index, 0, keepdims=False)
    up_weight_maps = lax.dynamic_index_in_dim(adapter_up_weight, tenant_index, 0, keepdims=False)
    low = jnp.dot(block_number, down_weight, preferred_element_type=jnp.float32).astype(jnp.bfloat16)
    low = low.astype(jnp.float32).reshape(BLOCK, 2, ADAPTER_RANK)
    return jnp.einsum("rhk,hkc->rhc", low, up_weight_maps.astype(jnp.float32)).astype(jnp.bfloat16)


def reference(hidden, key_value_weight, adapter_down_weight, adapter_up_weight, tenant_per_block):
    width = hidden.shape[1]
    piece = width // N_TP
    w_flat = key_value_weight.reshape(width, 2 * KEY_VALUE_WIDTH)
    base = jnp.zeros((TOKENS, 2 * KEY_VALUE_WIDTH), jnp.float32)
    for shard in range(N_TP):
        term = jnp.dot(hidden[:, shard * piece:(shard + 1) * piece], w_flat[shard * piece:(shard + 1) * piece], preferred_element_type=jnp.float32)
        base = base + lax.optimization_barrier(term.astype(jnp.bfloat16)).astype(jnp.float32)
    blocks = hidden.reshape(NBLK, BLOCK, width)

    def one_block(entry_list):
        return adapt_token_block(adapter_down_weight, adapter_up_weight, entry_list[0], entry_list[1])

    adapt = lax.map(one_block, (blocks, tenant_per_block.astype(jnp.int32)))
    total = base.reshape(TOKENS, 2, KEY_VALUE_WIDTH) + adapt.reshape(TOKENS, 2, KEY_VALUE_WIDTH).astype(jnp.float32)
    return total.astype(jnp.bfloat16)
```

```python
import jax
import jax.numpy as jnp
import numpy as np
from jax import lax
from jax.experimental import pallas as pl
from jax.experimental.pallas import tpu as pltpu
from jax.sharding import PartitionSpec as P

UNITS = 4
SCALE = 0.25
VMEM_BYTES = 63 * 1024 * 1024


def line_plan(n):
    sends = {}
    slots = np.zeros((n, n), np.int32)
    for i in range(n):
        order = []
        for c in range(n):
            if c == i:
                continue
            forward = c > i
            time = n - c + i if forward else c + n - i
            parity = (i if forward else i - 1) % 2
            order.append((time, 1 - parity, c, parity, i + 1 if forward else i - 1))
        order.sort()
        for k, (time, _, c, parity, to) in enumerate(order):
            slots[i, k] = c
            sends.setdefault((time, parity), []).append((i, to, k))
        slots[i, n - 1] = i
    return slots, sends


def by_device(table, axis):
    return jnp.asarray(table)[lax.axis_index(axis)]


def params():
    return pltpu.CompilerParams(vmem_limit_bytes=VMEM_BYTES)


def estimate(microseconds):
    return pl.CostEstimate(flops=1, bytes_accessed=int(microseconds * 3.69e6 * SCALE), transcendentals=0)


HERE = pl.BlockSpec(memory_space=pl.ANY)


def first_piece(hidden, weight, which, rows, chunk):
    width = hidden.shape[1]
    steps = 2
    depth = width // steps

    def body(which_ref, hidden_ref, weight_ref, flat_ref, out_ref, total):
        k = pl.program_id(0)
        flat_ref[...] = weight_ref[...].reshape(depth, 2 * chunk)
        term = jnp.dot(hidden_ref[...], flat_ref[...], preferred_element_type=jnp.float32)

        @pl.when(k == 0)
        def _():
            total[...] = term

        @pl.when(k > 0)
        def _():
            total[...] += term

        @pl.when(k == steps - 1)
        def _():
            out_ref[...] = total[...].astype(out_ref.dtype)

    return pl.pallas_call(
        body,
        name="first_piece",
        grid_spec=pltpu.PrefetchScalarGridSpec(
            num_scalar_prefetch=1,
            grid=(steps,),
            in_specs=[
                pl.BlockSpec((rows, depth), lambda k, c: (0, k)),
                pl.BlockSpec((depth, 2, chunk), lambda k, c: (k, 0, c[0])),
            ],
            out_specs=[
                pl.BlockSpec((depth, 2 * chunk), lambda k, c: (k, 0)),
                pl.BlockSpec((rows, 2 * chunk), lambda k, c: (0, 0)),
            ],
            scratch_shapes=[pltpu.VMEM((rows, 2 * chunk), jnp.float32)],
        ),
        out_shape=[
            jax.ShapeDtypeStruct((width, 2 * chunk), jnp.bfloat16),
            jax.ShapeDtypeStruct((rows, 2 * chunk), jnp.bfloat16),
        ],
        compiler_params=params(),
        cost_estimate=estimate(5.5),
    )(which, hidden, weight)


def row_outputs(cuts, block, columns):
    specs, shapes, places = [], [], []
    first = 0
    for rows in cuts:
        count = rows // block

        def index(i, first=first, count=count):
            return jnp.clip(i - first, 0, count - 1), 0

        specs.append((block, columns, index))
        shapes.append(jax.ShapeDtypeStruct((rows, columns), jnp.bfloat16))
        places.append((first, first + count))
        first += count
    return specs, shapes, places


def more_rows(hidden, flat, start, cuts, after):
    width, columns = flat.shape
    block = 512
    skip = start // block
    specs, shapes, places = row_outputs(cuts, block, columns)

    def body(hidden_ref, flat_ref, *refs):
        i = pl.program_id(0)
        value = jnp.dot(hidden_ref[...], flat_ref[...], preferred_element_type=jnp.float32).astype(jnp.bfloat16)
        for ref, (low, high) in zip(refs[len(after) :], places):

            @pl.when((i >= low) & (i < high))
            def _(ref=ref):
                ref[...] = value

    return pl.pallas_call(
        body,
        name="more_rows",
        grid=(sum(cuts) // block,),
        in_specs=[
            pl.BlockSpec((block, width), lambda i: (skip + i, 0)),
            pl.BlockSpec((width, columns), lambda i: (0, 0)),
        ]
        + [HERE] * len(after),
        out_specs=[pl.BlockSpec((b, c), index) for b, c, index in specs],
        out_shape=shapes,
        compiler_params=params(),
        cost_estimate=estimate(2.5 * sum(cuts) / block),
    )(hidden, flat, *after)


def other_slots(hidden, weight, which, cuts, chunk, after):
    tok_rows, width = hidden.shape
    count = len(cuts)
    steps = 4
    depth = width // steps
    block = 512
    out_specs, out_shapes, targets = [], [], []
    for slot_cuts in cuts:
        specs, shapes, places = row_outputs(slot_cuts, block, 2 * chunk)
        targets.append([(len(out_specs) + k, place) for k, place in enumerate(places)])
        for b, c, index in specs:
            out_specs.append(pl.BlockSpec((b, c), lambda i, w, index=index: index(i - steps)))
        out_shapes += shapes

    def body(which_ref, hidden_ref, *refs):
        weight_refs = refs[:count]
        outs = refs[count + len(after) : -1]
        flat = refs[-1]
        i = pl.program_id(0)

        @pl.when(i < steps)
        def _():
            for s in range(count):
                flat[s, pl.ds(pl.multiple_of(i * depth, depth), depth), :] = weight_refs[s][...].reshape(
                    depth, 2 * chunk
                )

        @pl.when(i >= steps)
        def _():
            for s in range(count):
                value = jnp.dot(hidden_ref[...], flat[s], preferred_element_type=jnp.float32).astype(jnp.bfloat16)
                for k, (low, high) in targets[s]:

                    @pl.when((i >= steps + low) & (i < steps + high))
                    def _(k=k, value=value):
                        outs[k][...] = value

    arrays = pl.pallas_call(
        body,
        name="other_slots",
        grid_spec=pltpu.PrefetchScalarGridSpec(
            num_scalar_prefetch=1,
            grid=(steps + tok_rows // block,),
            in_specs=[pl.BlockSpec((block, width), lambda i, w: (jnp.maximum(i - steps, 0), 0))]
            + [
                pl.BlockSpec((depth, 2, chunk), lambda i, w, s=s: (jnp.minimum(i, steps - 1), 0, w[s]))
                for s in range(count)
            ]
            + [HERE] * len(after),
            out_specs=out_specs,
            scratch_shapes=[pltpu.VMEM((count, width, 2 * chunk), jnp.bfloat16)],
        ),
        out_shape=out_shapes,
        compiler_params=params(),
        cost_estimate=estimate(8 + 1.3 * count * tok_rows / block),
    )(which, hidden, *[weight] * count, *after)
    return [[arrays[k] for k, _ in target] for target in targets]


def segment_specs(terms, start, block):
    specs, operands, layout = [], [], []
    for term in terms:
        places = []
        for first, array in term:
            count = array.shape[0] // block
            places.append((len(operands), (first - start) // block))
            operands.append(array)

            def index(i, *_, shift=(first - start) // block, count=count):
                return jnp.clip(i - shift, 0, count - 1), 0

            specs.append(pl.BlockSpec((block, array.shape[1]), index))
        layout.append(places)
    return specs, operands, layout


def term_sum(i, refs, layout):
    total = None
    for places in layout:
        value = refs[places[0][0]][...].astype(jnp.float32)
        for place, shift in places[1:]:
            value = jnp.where(i >= shift, refs[place][...].astype(jnp.float32), value)
        total = value if total is None else total + value
    return total


def added(start, rows, terms, after):
    columns = terms[0][0][1].shape[1]
    block = 512 if columns > 128 else rows
    specs, operands, layout = segment_specs(terms, start, block)

    def body(*refs):
        refs[-1][...] = term_sum(pl.program_id(0), refs, layout).astype(jnp.bfloat16)

    return pl.pallas_call(
        body,
        name="added",
        grid=(rows // block,),
        in_specs=specs + [HERE] * len(after),
        out_specs=pl.BlockSpec((block, columns), lambda i: (i, 0)),
        out_shape=jax.ShapeDtypeStruct((rows, columns), jnp.bfloat16),
        compiler_params=params(),
        cost_estimate=estimate(1.3 * rows * columns / 262144),
    )(*operands, *after)


def low_terms(hidden, down_maps, tenants, after):
    tok_rows, width = hidden.shape
    count = tenants.shape[0]
    rows = tok_rows // count
    columns = down_maps.shape[2]
    per = 4 if count % 4 == 0 else 1

    def body(tenant_ref, hidden_ref, *refs):
        for k in range(per):
            part = slice(k * rows, (k + 1) * rows)
            refs[-1][part, :] = jnp.dot(
                hidden_ref[part, :], refs[k][0], preferred_element_type=jnp.float32
            ).astype(jnp.bfloat16)

    return pl.pallas_call(
        body,
        name="low_terms",
        grid_spec=pltpu.PrefetchScalarGridSpec(
            num_scalar_prefetch=1,
            grid=(count // per,),
            in_specs=[pl.BlockSpec((per * rows, width), lambda b, t: (b, 0))]
            + [
                pl.BlockSpec((1, width, columns), lambda b, t, k=k: (t[b * per + k], 0, 0))
                for k in range(per)
            ]
            + [HERE] * len(after),
            out_specs=pl.BlockSpec((per * rows, columns), lambda b, t: (b, 0)),
        ),
        out_shape=jax.ShapeDtypeStruct((tok_rows, columns), jnp.bfloat16),
        compiler_params=params(),
        cost_estimate=estimate(8.6),
    )(tenants, hidden, *[down_maps] * per, *after)


def with_adapter(start, rows, terms, low_parts, up_maps, tenants, after):
    rank, chunk = up_maps.shape[2:]
    blk_rows = low_parts[0].shape[0] // tenants.shape[0]
    block = 512
    per = block // blk_rows
    skip = start // block
    specs, operands, layout = segment_specs(terms, start, block)
    n_low = len(low_parts)

    def body(tenant_ref, *refs):
        up_refs, low_refs, term_refs = refs[:per], refs[per : per + n_low], refs[per + n_low :]
        low = low_refs[0][...].astype(jnp.float32)
        for ref in low_refs[1:]:
            low = low + ref[...].astype(jnp.float32)
        low = low.astype(jnp.bfloat16)
        total = term_sum(pl.program_id(0), term_refs, layout)
        for k in range(per):
            part = slice(k * blk_rows, (k + 1) * blk_rows)
            for h in range(2):
                columns = slice(h * chunk, (h + 1) * chunk)
                adapt = jnp.dot(
                    low[part, h * rank : (h + 1) * rank], up_refs[k][0, h], preferred_element_type=jnp.float32
                )
                refs[-1][part, columns] = (total[part, columns] + adapt).astype(jnp.bfloat16)

    return pl.pallas_call(
        body,
        name="with_adapter",
        grid_spec=pltpu.PrefetchScalarGridSpec(
            num_scalar_prefetch=1,
            grid=(rows // block,),
            in_specs=[
                pl.BlockSpec((1, 2, rank, chunk), lambda b, t, k=k: (t[(skip + b) * per + k], 0, 0, 0))
                for k in range(per)
            ]
            + [pl.BlockSpec((block, 2 * rank), lambda b, t: (skip + b, 0)) for _ in low_parts]
            + specs
            + [HERE] * len(after),
            out_specs=pl.BlockSpec((block, 2 * chunk), lambda b, t: (b, 0)),
        ),
        out_shape=jax.ShapeDtypeStruct((rows, 2 * chunk), jnp.bfloat16),
        compiler_params=params(),
        cost_estimate=estimate(2 * rows / block),
    )(tenants, *[up_maps] * per, *low_parts, *operands, *after)


def finish(start, rows, out_rows, terms, previous):
    chunk = terms[0][0][1].shape[1] // 2
    block = 512
    skip = start // block
    specs, operands, layout = segment_specs(terms, start, block)
    aliases = {}
    if previous is not None:
        aliases = {len(operands): 0}
        specs.append(HERE)
        operands.append(previous)

    def body(*refs):
        total = term_sum(pl.program_id(0), refs, layout)
        refs[-1][...] = total.astype(jnp.bfloat16).reshape(block, 2, chunk)

    return pl.pallas_call(
        body,
        name="finish",
        grid=(rows // block,),
        in_specs=specs,
        out_specs=pl.BlockSpec((block, 2, chunk), lambda i: (skip + i, 0, 0)),
        out_shape=jax.ShapeDtypeStruct((out_rows, 2, chunk), jnp.bfloat16),
        input_output_aliases=aliases,
        compiler_params=params(),
        cost_estimate=estimate(1.3 * rows / block),
    )(*operands)


def local(n, hidden, key_value_weight, adapter_down_weight, adapter_up_weight, tenant_per_block):
    tok_rows, local_width = hidden.shape
    chunk = adapter_up_weight.shape[3]
    unit = tok_rows // UNITS
    slots, sends = line_plan(n)

    down_maps = lax.all_gather(adapter_down_weight, "tok", axis=0, tiled=True)
    up_maps = lax.all_gather(adapter_up_weight, "tok", axis=0, tiled=True)

    which = by_device(slots, "tp")
    partial = {}
    received = {}
    last = []

    def pick(segments, start, rows):
        return [(f, a) for f, a in segments if f < start + rows and start < f + a.shape[0]]

    def ordered(array):
        last[:] = [array]
        return array

    def cut(arrays, start=0):
        segments = []
        for array in arrays:
            segments.append((start, array))
            start += array.shape[0]
        return segments

    def send(time, parity, u, count, after=(), again=False):
        start, rows = u * unit, count * unit
        ks = sorted({k for _, _, k in sends[time, parity]})
        earlier = pick(received.get((time - 1, 1 - parity), []), start, rows)
        own = pick(partial[ks[0]], start, rows)
        if len(ks) > 1:
            table = np.zeros((n,), np.int32)
            for i, _, k in sends[time, parity]:
                table[i] = k
            mine = by_device(table, "tp")
            ((_, value),) = own
            for k in ks[1:]:
                ((_, other),) = pick(partial[k], start, rows)
                value = jnp.where(mine == k, other, value)
            own = [(start, value)]
        if earlier or again:
            terms = [own, earlier] if earlier else [own]
            value = ordered(added(start, rows, terms, last + list(after)))
        else:
            ((_, value),) = own
        moves = [(i, to) for i, to, _ in sends[time, parity]]
        with jax.named_scope(f"{'odd' if parity else 'even'}{time}_units{u}"):
            moved = lax.ppermute(value, "tp", moves)
        received.setdefault((time, parity), []).append((start, moved))
        return received[time, parity][-1][1]

    low_parts = []

    def send_low(time):
        value = low_parts[0]
        if time > 1:
            value = ordered(added(0, tok_rows, [[(0, value)], [(0, low_parts[-1])]], list(last)))
        with jax.named_scope(f"low_sums{time}"):
            low_parts.append(lax.ppermute(value, "tp", [(time - 1, time), (n - time, n - time - 1)]))

    ready = []

    def prepare(u, count):
        start, rows = u * unit, count * unit
        terms = [pick(partial[n - 1], start, rows), pick(received[n - 1, 1], start, rows)]
        value = with_adapter(start, rows, terms, low_parts, up_maps, tenant_per_block, list(last))
        ready.append((start, ordered(value)))

    result = [None]

    def complete(u, count):
        start, rows = u * unit, count * unit
        terms = [pick(ready, start, rows), pick(received[n - 1, 0], start, rows)]
        result[0] = finish(start, rows, tok_rows, terms, result[0])

    half = UNITS // 2
    flat, head = first_piece(hidden, key_value_weight, which[:1], half * unit, chunk)
    partial[0] = [(0, head)]
    if n == 4:
        send(1, 0, 0, 2)
        partial[0] += cut(more_rows(hidden, flat, half * unit, [half * unit], []), half * unit)
        send(1, 0, 2, 2)
        others = other_slots(
            hidden, key_value_weight, which[1:], [[2 * unit, 2 * unit], [tok_rows], [tok_rows]], chunk, [partial[0][1][1]]
        )
        for s, arrays in enumerate(others):
            partial[s + 1] = cut(arrays)
        ordered(partial[3][0][1])
        send(2, 0, 0, 2)
        send(2, 1, 0, 2)
        send(2, 1, 2, 2)
        low_parts.append(ordered(low_terms(hidden, down_maps, tenant_per_block, list(last))))
        send_low(1)
        send(2, 0, 2, 2, again=True)
        send(3, 1, 0, 2)
        send(3, 0, 0, 2)
        send_low(2)
        send(3, 0, 2, 1)
        send_low(3)
        send(3, 1, 2, 2)
        send(3, 0, 3, 1)
        prepare(0, 2)
        complete(0, 2)
        prepare(2, 2)
        complete(2, 1)
        complete(3, 1)
    else:
        partial[0] = [
            (0, jnp.concatenate([head] + list(more_rows(hidden, flat, half * unit, [half * unit], []))))
        ]
        others = other_slots(hidden, key_value_weight, which[1:], [[tok_rows]] * (n - 1), chunk, [head])
        for s, arrays in enumerate(others):
            partial[s + 1] = cut(arrays)
        ordered(head)
        for time in range(1, n):
            for parity in (0, 1):
                if (time, parity) in sends:
                    send(time, parity, 0, UNITS)
        low_parts.append(ordered(low_terms(hidden, down_maps, tenant_per_block, list(last))))
        for time in range(1, n):
            send_low(time)
        prepare(0, UNITS)
        complete(0, UNITS)
    return result[0]


def solution(mesh):
    n = mesh.shape["tp"]
    in_specs = (
        P("tok", "tp"),
        P("tp", None, None),
        P("tok", "tp", None),
        P("tok", None, None, "tp"),
        P("tok"),
    )
    out_specs = P("tok", None, "tp")

    def run(*args):
        return local(n, *args)

    return jax.shard_map(run, mesh=mesh, in_specs=in_specs, out_specs=out_specs, check_vma=False)
```

```python
import jax
import jax.numpy as jnp
import numpy as np
from jax import lax
from jax.experimental import pallas as pl
from jax.experimental.pallas import tpu as pltpu
from jax.sharding import PartitionSpec as P

UNITS = 8
SCALE = 0.25
VMEM_BYTES = 64 * 1024 * 1024 - 256 * 1024


def line_plan(n):
    sends = {}
    slots = np.zeros((n, n), np.int32)
    for i in range(n):
        order = []
        for c in range(n):
            if c == i:
                continue
            forward = c > i
            time = n - c + i if forward else c + n - i
            parity = (i if forward else i - 1) % 2
            order.append((time, 1 - parity, c, parity, i + 1 if forward else i - 1))
        order.sort()
        for k, (time, _, c, parity, to) in enumerate(order):
            slots[i, k] = c
            sends.setdefault((time, parity), []).append((i, to, k))
        slots[i, n - 1] = i
    return slots, sends


def by_device(table, axis):
    return jnp.asarray(table)[lax.axis_index(axis)]


def chunk_of(table, place):
    value = int(table[0])
    for i in range(1, len(table)):
        value = jnp.where(place == i, int(table[i]), value)
    return value


def params():
    return pltpu.CompilerParams(vmem_limit_bytes=VMEM_BYTES)


def estimate(microseconds):
    return pl.CostEstimate(flops=1, bytes_accessed=int(microseconds * 3.69e6 * SCALE), transcendentals=0)


HERE = pl.BlockSpec(memory_space=pl.ANY)


def first_piece(hidden, weight, place, which, rows, chunk):
    width = hidden.shape[1]
    steps = 2
    depth = width // steps

    def body(which_ref, hidden_ref, weight_ref, flat_ref, out_ref, total):
        k = pl.program_id(0)
        flat_ref[...] = weight_ref[...].reshape(depth, 2 * chunk)
        term = jnp.dot(hidden_ref[...], flat_ref[...], preferred_element_type=jnp.float32)

        @pl.when(k == 0)
        def _():
            total[...] = term

        @pl.when(k > 0)
        def _():
            total[...] += term

        @pl.when(k == steps - 1)
        def _():
            out_ref[...] = total[...].astype(out_ref.dtype)

    return pl.pallas_call(
        body,
        name="first_piece",
        grid_spec=pltpu.PrefetchScalarGridSpec(
            num_scalar_prefetch=1,
            grid=(steps,),
            in_specs=[
                pl.BlockSpec((rows, depth), lambda k, c: (0, k)),
                pl.BlockSpec((depth, 2, chunk), lambda k, c: (k, 0, chunk_of(which, c[0]))),
            ],
            out_specs=[
                pl.BlockSpec((depth, 2 * chunk), lambda k, c: (k, 0)),
                pl.BlockSpec((rows, 2 * chunk), lambda k, c: (0, 0)),
            ],
            scratch_shapes=[pltpu.VMEM((rows, 2 * chunk), jnp.float32)],
        ),
        out_shape=[
            jax.ShapeDtypeStruct((width, 2 * chunk), jnp.bfloat16),
            jax.ShapeDtypeStruct((rows, 2 * chunk), jnp.bfloat16),
        ],
        compiler_params=params(),
        cost_estimate=estimate(5.5),
    )(place, hidden, weight)


def row_outputs(cuts, block, columns):
    specs, shapes, places = [], [], []
    first = 0
    for rows in cuts:
        count = rows // block

        def index(i, first=first, count=count):
            return jnp.clip(i - first, 0, count - 1), 0

        specs.append((block, columns, index))
        shapes.append(jax.ShapeDtypeStruct((rows, columns), jnp.bfloat16))
        places.append((first, first + count))
        first += count
    return specs, shapes, places


def more_rows(hidden, flat, start, cuts, after):
    width, columns = flat.shape
    block = 512
    skip = start // block
    specs, shapes, places = row_outputs(cuts, block, columns)

    def body(hidden_ref, flat_ref, *refs):
        i = pl.program_id(0)
        value = jnp.dot(hidden_ref[...], flat_ref[...], preferred_element_type=jnp.float32).astype(jnp.bfloat16)
        for ref, (low, high) in zip(refs[len(after) :], places):

            @pl.when((i >= low) & (i < high))
            def _(ref=ref):
                ref[...] = value

    return pl.pallas_call(
        body,
        name="more_rows",
        grid=(sum(cuts) // block,),
        in_specs=[
            pl.BlockSpec((block, width), lambda i: (skip + i, 0)),
            pl.BlockSpec((width, columns), lambda i: (0, 0)),
        ]
        + [HERE] * len(after),
        out_specs=[pl.BlockSpec((b, c), index) for b, c, index in specs],
        out_shape=shapes,
        compiler_params=params(),
        cost_estimate=estimate(2.5 * sum(cuts) / block),
    )(hidden, flat, *after)


def other_slots(hidden, weight, place, which, cuts, chunk, after):
    tok_rows, width = hidden.shape
    count = len(cuts)
    steps = 4
    depth = width // steps
    block = 512
    out_specs, out_shapes, targets = [], [], []
    for slot_cuts in cuts:
        specs, shapes, places = row_outputs(slot_cuts, block, 2 * chunk)
        targets.append([(len(out_specs) + k, place) for k, place in enumerate(places)])
        for b, c, index in specs:
            out_specs.append(pl.BlockSpec((b, c), lambda i, w, index=index: index(i - steps)))
        out_shapes += shapes

    def body(which_ref, hidden_ref, *refs):
        weight_refs = refs[:count]
        outs = refs[count + len(after) : -1]
        flat = refs[-1]
        i = pl.program_id(0)

        @pl.when(i < steps)
        def _():
            for s in range(count):
                flat[s, pl.ds(pl.multiple_of(i * depth, depth), depth), :] = weight_refs[s][...].reshape(
                    depth, 2 * chunk
                )

        @pl.when(i >= steps)
        def _():
            for s in range(count):
                value = jnp.dot(hidden_ref[...], flat[s], preferred_element_type=jnp.float32).astype(jnp.bfloat16)
                for k, (low, high) in targets[s]:

                    @pl.when((i >= steps + low) & (i < steps + high))
                    def _(k=k, value=value):
                        outs[k][...] = value

    arrays = pl.pallas_call(
        body,
        name="other_slots",
        grid_spec=pltpu.PrefetchScalarGridSpec(
            num_scalar_prefetch=1,
            grid=(steps + tok_rows // block,),
            in_specs=[pl.BlockSpec((block, width), lambda i, w: (jnp.maximum(i - steps, 0), 0))]
            + [
                pl.BlockSpec((depth, 2, chunk), lambda i, w, s=s: (jnp.minimum(i, steps - 1), 0, chunk_of(which[s], w[0])))
                for s in range(count)
            ]
            + [HERE] * len(after),
            out_specs=out_specs,
            scratch_shapes=[pltpu.VMEM((count, width, 2 * chunk), jnp.bfloat16)],
        ),
        out_shape=out_shapes,
        compiler_params=params(),
        cost_estimate=estimate(8 + 1.3 * count * tok_rows / block),
    )(place, hidden, *[weight] * count, *after)
    return [[arrays[k] for k, _ in target] for target in targets]


def segment_specs(terms, start, block):
    specs, operands, layout = [], [], []
    for term in terms:
        places = []
        for first, array in term:
            count = array.shape[0] // block
            places.append((len(operands), (first - start) // block))
            operands.append(array)

            def index(i, *_, shift=(first - start) // block, count=count):
                return jnp.clip(i - shift, 0, count - 1), 0

            specs.append(pl.BlockSpec((block, array.shape[1]), index))
        layout.append(places)
    return specs, operands, layout


def term_sum(i, refs, layout):
    total = None
    for places in layout:
        value = refs[places[0][0]][...].astype(jnp.float32)
        for place, shift in places[1:]:
            value = jnp.where(i >= shift, refs[place][...].astype(jnp.float32), value)
        total = value if total is None else total + value
    return total


def added(start, rows, terms, after):
    columns = terms[0][0][1].shape[1]
    block = rows if columns <= 128 else 512 if rows % 512 == start % 512 == 0 else 256
    specs, operands, layout = segment_specs(terms, start, block)

    def body(*refs):
        refs[-1][...] = term_sum(pl.program_id(0), refs, layout).astype(jnp.bfloat16)

    return pl.pallas_call(
        body,
        name="added",
        grid=(rows // block,),
        in_specs=specs + [HERE] * len(after),
        out_specs=pl.BlockSpec((block, columns), lambda i: (i, 0)),
        out_shape=jax.ShapeDtypeStruct((rows, columns), jnp.bfloat16),
        compiler_params=params(),
        cost_estimate=estimate(1.3 * rows * columns / 262144),
    )(*operands, *after)


def low_terms(hidden, down_maps, tenants, after):
    tok_rows, width = hidden.shape
    count = tenants.shape[0]
    rows = tok_rows // count
    columns = down_maps.shape[2]
    per = 4 if count % 4 == 0 else 1

    def body(tenant_ref, hidden_ref, *refs):
        for k in range(per):
            part = slice(k * rows, (k + 1) * rows)
            refs[-1][part, :] = jnp.dot(
                hidden_ref[part, :], refs[k][0], preferred_element_type=jnp.float32
            ).astype(jnp.bfloat16)

    return pl.pallas_call(
        body,
        name="low_terms",
        grid_spec=pltpu.PrefetchScalarGridSpec(
            num_scalar_prefetch=1,
            grid=(count // per,),
            in_specs=[pl.BlockSpec((per * rows, width), lambda b, t: (b, 0))]
            + [
                pl.BlockSpec((1, width, columns), lambda b, t, k=k: (t[b * per + k], 0, 0))
                for k in range(per)
            ]
            + [HERE] * len(after),
            out_specs=pl.BlockSpec((per * rows, columns), lambda b, t: (b, 0)),
        ),
        out_shape=jax.ShapeDtypeStruct((tok_rows, columns), jnp.bfloat16),
        compiler_params=params(),
        cost_estimate=estimate(8.6),
    )(tenants, hidden, *[down_maps] * per, *after)


def with_adapter(start, rows, terms, low_parts, up_maps, tenants, after):
    rank, chunk = up_maps.shape[2:]
    blk_rows = low_parts[0].shape[0] // tenants.shape[0]
    block = 512
    per = block // blk_rows
    skip = start // block
    specs, operands, layout = segment_specs(terms, start, block)
    n_low = len(low_parts)

    def body(tenant_ref, *refs):
        up_refs, low_refs, term_refs = refs[:per], refs[per : per + n_low], refs[per + n_low :]
        low = low_refs[0][...].astype(jnp.float32)
        for ref in low_refs[1:]:
            low = low + ref[...].astype(jnp.float32)
        low = low.astype(jnp.bfloat16)
        total = term_sum(pl.program_id(0), term_refs, layout)
        for k in range(per):
            part = slice(k * blk_rows, (k + 1) * blk_rows)
            for h in range(2):
                columns = slice(h * chunk, (h + 1) * chunk)
                adapt = jnp.dot(
                    low[part, h * rank : (h + 1) * rank], up_refs[k][0, h], preferred_element_type=jnp.float32
                )
                refs[-1][part, columns] = (total[part, columns] + adapt).astype(jnp.bfloat16)

    return pl.pallas_call(
        body,
        name="with_adapter",
        grid_spec=pltpu.PrefetchScalarGridSpec(
            num_scalar_prefetch=1,
            grid=(rows // block,),
            in_specs=[
                pl.BlockSpec((1, 2, rank, chunk), lambda b, t, k=k: (t[(skip + b) * per + k], 0, 0, 0))
                for k in range(per)
            ]
            + [pl.BlockSpec((block, 2 * rank), lambda b, t: (skip + b, 0)) for _ in low_parts]
            + specs
            + [HERE] * len(after),
            out_specs=pl.BlockSpec((block, 2 * chunk), lambda b, t: (b, 0)),
        ),
        out_shape=jax.ShapeDtypeStruct((rows, 2 * chunk), jnp.bfloat16),
        compiler_params=params(),
        cost_estimate=estimate(2 * rows / block),
    )(tenants, *[up_maps] * per, *low_parts, *operands, *after)


def finish(start, rows, out_rows, terms, previous):
    chunk = terms[0][0][1].shape[1] // 2
    block = 512 if rows % 512 == start % 512 == 0 else 256
    skip = start // block
    specs, operands, layout = segment_specs(terms, start, block)
    aliases = {}
    if previous is not None:
        aliases = {len(operands): 0}
        specs.append(HERE)
        operands.append(previous)

    def body(*refs):
        total = term_sum(pl.program_id(0), refs, layout)
        refs[-1][...] = total.astype(jnp.bfloat16).reshape(block, 2, chunk)

    return pl.pallas_call(
        body,
        name="finish",
        grid=(rows // block,),
        in_specs=specs,
        out_specs=pl.BlockSpec((block, 2, chunk), lambda i: (skip + i, 0, 0)),
        out_shape=jax.ShapeDtypeStruct((out_rows, 2, chunk), jnp.bfloat16),
        input_output_aliases=aliases,
        compiler_params=params(),
        cost_estimate=estimate(1.3 * rows / block),
    )(*operands)


def local(n, hidden, key_value_weight, adapter_down_weight, adapter_up_weight, tenant_per_block):
    tok_rows, local_width = hidden.shape
    chunk = adapter_up_weight.shape[3]
    unit = tok_rows // UNITS
    slots, sends = line_plan(n)

    down_maps = lax.all_gather(adapter_down_weight, "tok", axis=0, tiled=True)
    up_maps = lax.all_gather(adapter_up_weight, "tok", axis=0, tiled=True)

    place = lax.axis_index("tp").reshape(1)
    which = slots.T
    partial = {}
    received = {}
    last = []

    def pick(segments, start, rows):
        return [(f, a) for f, a in segments if f < start + rows and start < f + a.shape[0]]

    def ordered(array):
        last[:] = [array]
        return array

    def cut(arrays, start=0):
        segments = []
        for array in arrays:
            segments.append((start, array))
            start += array.shape[0]
        return segments

    def send(time, parity, u, count, after=(), again=False):
        start, rows = u * unit, count * unit
        ks = sorted({k for _, _, k in sends[time, parity]})
        earlier = pick(received.get((time - 1, 1 - parity), []), start, rows)
        own = pick(partial[ks[0]], start, rows)
        if len(ks) > 1:
            table = np.zeros((n,), np.int32)
            for i, _, k in sends[time, parity]:
                table[i] = k
            mine = by_device(table, "tp")
            ((_, value),) = own
            for k in ks[1:]:
                ((_, other),) = pick(partial[k], start, rows)
                value = jnp.where(mine == k, other, value)
            own = [(start, value)]
        if earlier or again:
            terms = [own, earlier] if earlier else [own]
            value = ordered(added(start, rows, terms, last + list(after)))
        else:
            ((_, value),) = own
        moves = [(i, to) for i, to, _ in sends[time, parity]]
        with jax.named_scope(f"{'odd' if parity else 'even'}{time}_units{u}"):
            moved = lax.ppermute(value, "tp", moves)
        received.setdefault((time, parity), []).append((start, moved))
        return received[time, parity][-1][1]

    low_parts = []

    def send_low(time, after=()):
        value = low_parts[0]
        if time > 1:
            value = ordered(added(0, tok_rows, [[(0, value)], [(0, low_parts[-1])]], last + list(after)))
        with jax.named_scope(f"low_sums{time}"):
            low_parts.append(lax.ppermute(value, "tp", [(time - 1, time), (n - time, n - time - 1)]))

    ready = []

    def prepare(u, count):
        start, rows = u * unit, count * unit
        terms = [pick(partial[n - 1], start, rows)]
        value = with_adapter(start, rows, terms, low_parts, up_maps, tenant_per_block, list(last))
        ready.append((start, ordered(value)))

    result = [None]

    def complete(u, count):
        start, rows = u * unit, count * unit
        terms = [pick(ready, start, rows)] + [pick(received[n - 1, parity], start, rows) for parity in (0, 1)]
        result[0] = finish(start, rows, tok_rows, terms, result[0])

    first = 2 * unit
    flat, head = first_piece(hidden, key_value_weight, place, which[0], first, chunk)
    partial[0] = [(0, head)]
    if n == 4:
        arrived = send(1, 0, 0, 2)
        partial[0] += cut(more_rows(hidden, flat, first, [first] * 3, []), first)
        for u in (2, 4, 6):
            send(1, 0, u, 2)
        others = other_slots(
            hidden,
            key_value_weight,
            place,
            which[1:],
            [[tok_rows // 2] * 2, [tok_rows], [tok_rows]],
            chunk,
            [partial[0][-1][1], arrived],
        )
        for s, arrays in enumerate(others):
            partial[s + 1] = cut(arrays)
        ordered(partial[3][0][1])
        send(2, 0, 0, 4)
        send(2, 1, 0, 4)
        send(2, 1, 4, 4)
        low_parts.append(ordered(low_terms(hidden, down_maps, tenant_per_block, list(last))))
        send_low(1)
        send(2, 0, 4, 4, again=True)
        send(3, 1, 0, 4)
        send(3, 0, 0, 4)
        send_low(2)
        send(3, 0, 4, 2)
        send_low(3)
        send(3, 1, 4, 4)
        send(3, 0, 6, 2)
        prepare(0, 8)
        complete(0, 4)
        complete(4, 2)
        complete(6, 2)
    else:
        partial[0] = [
            (0, jnp.concatenate([head] + list(more_rows(hidden, flat, first, [tok_rows - first], []))))
        ]
        others = other_slots(hidden, key_value_weight, place, which[1:], [[tok_rows]] * (n - 1), chunk, [head])
        for s, arrays in enumerate(others):
            partial[s + 1] = cut(arrays)
        ordered(head)
        for time in range(1, n):
            for parity in (0, 1):
                if (time, parity) in sends:
                    send(time, parity, 0, UNITS)
        low_parts.append(ordered(low_terms(hidden, down_maps, tenant_per_block, list(last))))
        for time in range(1, n):
            send_low(time)
        prepare(0, UNITS)
        complete(0, UNITS)
    return result[0]


def solution(mesh):
    n = mesh.shape["tp"]
    in_specs = (
        P("tok", "tp"),
        P("tp", None, None),
        P("tok", "tp", None),
        P("tok", None, None, "tp"),
        P("tok"),
    )
    out_specs = P("tok", None, "tp")

    def run(*args):
        return local(n, *args)

    return jax.shard_map(run, mesh=mesh, in_specs=in_specs, out_specs=out_specs, check_vma=False)
```

```python
import jax
import jax.numpy as jnp
import numpy as np
from jax import lax
from jax.experimental import pallas as pl
from jax.experimental.pallas import tpu as pltpu
from jax.sharding import PartitionSpec as P

UNITS = 8
SCALE = 0.25
VMEM_BYTES = 64 * 1024 * 1024 - 256 * 1024


def line_plan(n):
    sends = {}
    slots = np.zeros((n, n), np.int32)
    for i in range(n):
        order = []
        for c in range(n):
            if c == i:
                continue
            forward = c > i
            time = n - c + i if forward else c + n - i
            parity = (i if forward else i - 1) % 2
            order.append((time, 1 - parity, c, parity, i + 1 if forward else i - 1))
        order.sort()
        for k, (time, _, c, parity, to) in enumerate(order):
            slots[i, k] = c
            sends.setdefault((time, parity), []).append((i, to, k))
        slots[i, n - 1] = i
    return slots, sends


def by_device(table, axis):
    return jnp.asarray(table)[lax.axis_index(axis)]


def chunk_of(table, place):
    value = int(table[0])
    for i in range(1, len(table)):
        value = jnp.where(place == i, int(table[i]), value)
    return value


def params():
    return pltpu.CompilerParams(vmem_limit_bytes=VMEM_BYTES)


def estimate(microseconds):
    return pl.CostEstimate(flops=1, bytes_accessed=int(microseconds * 3.69e6 * SCALE), transcendentals=0)


HERE = pl.BlockSpec(memory_space=pl.ANY)


def first_piece(hidden, weight, place, which, rows, chunk):
    width = hidden.shape[1]
    steps = 2
    depth = width // steps

    def body(which_ref, hidden_ref, weight_ref, flat_ref, out_ref, total):
        k = pl.program_id(0)
        flat_ref[...] = weight_ref[...].reshape(depth, 2 * chunk)
        term = jnp.dot(hidden_ref[...], flat_ref[...], preferred_element_type=jnp.float32)

        @pl.when(k == 0)
        def _():
            total[...] = term

        @pl.when(k > 0)
        def _():
            total[...] += term

        @pl.when(k == steps - 1)
        def _():
            out_ref[...] = total[...].astype(out_ref.dtype)

    return pl.pallas_call(
        body,
        name="first_piece",
        grid_spec=pltpu.PrefetchScalarGridSpec(
            num_scalar_prefetch=1,
            grid=(steps,),
            in_specs=[
                pl.BlockSpec((rows, depth), lambda k, c: (0, k)),
                pl.BlockSpec((depth, 2, chunk), lambda k, c: (k, 0, chunk_of(which, c[0]))),
            ],
            out_specs=[
                pl.BlockSpec((depth, 2 * chunk), lambda k, c: (k, 0)),
                pl.BlockSpec((rows, 2 * chunk), lambda k, c: (0, 0)),
            ],
            scratch_shapes=[pltpu.VMEM((rows, 2 * chunk), jnp.float32)],
        ),
        out_shape=[
            jax.ShapeDtypeStruct((width, 2 * chunk), jnp.bfloat16),
            jax.ShapeDtypeStruct((rows, 2 * chunk), jnp.bfloat16),
        ],
        compiler_params=params(),
        cost_estimate=estimate(5.5),
    )(place, hidden, weight)


def row_outputs(cuts, block, columns):
    specs, shapes, places = [], [], []
    first = 0
    for rows in cuts:
        count = rows // block

        def index(i, first=first, count=count):
            return jnp.clip(i - first, 0, count - 1), 0

        specs.append((block, columns, index))
        shapes.append(jax.ShapeDtypeStruct((rows, columns), jnp.bfloat16))
        places.append((first, first + count))
        first += count
    return specs, shapes, places


def more_rows(hidden, flat, start, cuts, after):
    width, columns = flat.shape
    block = 512
    skip = start // block
    specs, shapes, places = row_outputs(cuts, block, columns)

    def body(hidden_ref, flat_ref, *refs):
        i = pl.program_id(0)
        value = jnp.dot(hidden_ref[...], flat_ref[...], preferred_element_type=jnp.float32).astype(jnp.bfloat16)
        for ref, (low, high) in zip(refs[len(after) :], places):

            @pl.when((i >= low) & (i < high))
            def _(ref=ref):
                ref[...] = value

    return pl.pallas_call(
        body,
        name="more_rows",
        grid=(sum(cuts) // block,),
        in_specs=[
            pl.BlockSpec((block, width), lambda i: (skip + i, 0)),
            pl.BlockSpec((width, columns), lambda i: (0, 0)),
        ]
        + [HERE] * len(after),
        out_specs=[pl.BlockSpec((b, c), index) for b, c, index in specs],
        out_shape=shapes,
        compiler_params=params(),
        cost_estimate=estimate(2.5 * sum(cuts) / block),
    )(hidden, flat, *after)


def other_slots(hidden, weight, place, which, cuts, chunk, after):
    tok_rows, width = hidden.shape
    count = len(cuts)
    steps = 4
    depth = width // steps
    block = 512
    out_specs, out_shapes, targets = [], [], []
    for slot_cuts in cuts:
        specs, shapes, places = row_outputs(slot_cuts, block, 2 * chunk)
        targets.append([(len(out_specs) + k, place) for k, place in enumerate(places)])
        for b, c, index in specs:
            out_specs.append(pl.BlockSpec((b, c), lambda i, w, index=index: index(i - steps)))
        out_shapes += shapes

    def body(which_ref, hidden_ref, *refs):
        weight_refs = refs[:count]
        outs = refs[count + len(after) : -1]
        flat = refs[-1]
        i = pl.program_id(0)

        @pl.when(i < steps)
        def _():
            for s in range(count):
                flat[s, pl.ds(pl.multiple_of(i * depth, depth), depth), :] = weight_refs[s][...].reshape(
                    depth, 2 * chunk
                )

        @pl.when(i >= steps)
        def _():
            for s in range(count):
                value = jnp.dot(hidden_ref[...], flat[s], preferred_element_type=jnp.float32).astype(jnp.bfloat16)
                for k, (low, high) in targets[s]:

                    @pl.when((i >= steps + low) & (i < steps + high))
                    def _(k=k, value=value):
                        outs[k][...] = value

    arrays = pl.pallas_call(
        body,
        name="other_slots",
        grid_spec=pltpu.PrefetchScalarGridSpec(
            num_scalar_prefetch=1,
            grid=(steps + tok_rows // block,),
            in_specs=[pl.BlockSpec((block, width), lambda i, w: (jnp.maximum(i - steps, 0), 0))]
            + [
                pl.BlockSpec((depth, 2, chunk), lambda i, w, s=s: (jnp.minimum(i, steps - 1), 0, chunk_of(which[s], w[0])))
                for s in range(count)
            ]
            + [HERE] * len(after),
            out_specs=out_specs,
            scratch_shapes=[pltpu.VMEM((count, width, 2 * chunk), jnp.bfloat16)],
        ),
        out_shape=out_shapes,
        compiler_params=params(),
        cost_estimate=estimate(8 + 1.3 * count * tok_rows / block),
    )(place, hidden, *[weight] * count, *after)
    return [[arrays[k] for k, _ in target] for target in targets]


def segment_specs(terms, start, block):
    specs, operands, layout = [], [], []
    for term in terms:
        places = []
        for first, array in term:
            count = array.shape[0] // block
            places.append((len(operands), (first - start) // block))
            operands.append(array)

            def index(i, *_, shift=(first - start) // block, count=count):
                return jnp.clip(i - shift, 0, count - 1), 0

            specs.append(pl.BlockSpec((block, array.shape[1]), index))
        layout.append(places)
    return specs, operands, layout


def term_sum(i, refs, layout):
    total = None
    for places in layout:
        value = refs[places[0][0]][...].astype(jnp.float32)
        for place, shift in places[1:]:
            value = jnp.where(i >= shift, refs[place][...].astype(jnp.float32), value)
        total = value if total is None else total + value
    return total


def added(start, rows, terms, after):
    columns = terms[0][0][1].shape[1]
    block = rows if columns <= 128 else 512 if rows % 512 == start % 512 == 0 else 256
    specs, operands, layout = segment_specs(terms, start, block)

    def body(*refs):
        refs[-1][...] = term_sum(pl.program_id(0), refs, layout).astype(jnp.bfloat16)

    return pl.pallas_call(
        body,
        name="added",
        grid=(rows // block,),
        in_specs=specs + [HERE] * len(after),
        out_specs=pl.BlockSpec((block, columns), lambda i: (i, 0)),
        out_shape=jax.ShapeDtypeStruct((rows, columns), jnp.bfloat16),
        compiler_params=params(),
        cost_estimate=estimate(1.3 * rows * columns / 262144),
    )(*operands, *after)


def low_terms(hidden, down_maps, tenants, after):
    tok_rows, width = hidden.shape
    count = tenants.shape[0]
    rows = tok_rows // count
    columns = down_maps.shape[2]
    per = 4 if count % 4 == 0 else 1

    def body(tenant_ref, hidden_ref, *refs):
        for k in range(per):
            part = slice(k * rows, (k + 1) * rows)
            refs[-1][part, :] = jnp.dot(
                hidden_ref[part, :], refs[k][0], preferred_element_type=jnp.float32
            ).astype(jnp.bfloat16)

    return pl.pallas_call(
        body,
        name="low_terms",
        grid_spec=pltpu.PrefetchScalarGridSpec(
            num_scalar_prefetch=1,
            grid=(count // per,),
            in_specs=[pl.BlockSpec((per * rows, width), lambda b, t: (b, 0))]
            + [
                pl.BlockSpec((1, width, columns), lambda b, t, k=k: (t[b * per + k], 0, 0))
                for k in range(per)
            ]
            + [HERE] * len(after),
            out_specs=pl.BlockSpec((per * rows, columns), lambda b, t: (b, 0)),
        ),
        out_shape=jax.ShapeDtypeStruct((tok_rows, columns), jnp.bfloat16),
        compiler_params=params(),
        cost_estimate=estimate(8.6),
    )(tenants, hidden, *[down_maps] * per, *after)


def with_adapter(start, rows, terms, low_parts, up_maps, tenants, after):
    rank, chunk = up_maps.shape[2:]
    blk_rows = low_parts[0].shape[0] // tenants.shape[0]
    block = 512
    per = block // blk_rows
    skip = start // block
    specs, operands, layout = segment_specs(terms, start, block)
    n_low = len(low_parts)

    def body(tenant_ref, *refs):
        up_refs, low_refs, term_refs = refs[:per], refs[per : per + n_low], refs[per + n_low :]
        low = low_refs[0][...].astype(jnp.float32)
        for ref in low_refs[1:]:
            low = low + ref[...].astype(jnp.float32)
        low = low.astype(jnp.bfloat16)
        total = term_sum(pl.program_id(0), term_refs, layout)
        for k in range(per):
            part = slice(k * blk_rows, (k + 1) * blk_rows)
            for h in range(2):
                columns = slice(h * chunk, (h + 1) * chunk)
                adapt = jnp.dot(
                    low[part, h * rank : (h + 1) * rank], up_refs[k][0, h], preferred_element_type=jnp.float32
                )
                refs[-1][part, columns] = (total[part, columns] + adapt).astype(jnp.bfloat16)

    return pl.pallas_call(
        body,
        name="with_adapter",
        grid_spec=pltpu.PrefetchScalarGridSpec(
            num_scalar_prefetch=1,
            grid=(rows // block,),
            in_specs=[
                pl.BlockSpec((1, 2, rank, chunk), lambda b, t, k=k: (t[(skip + b) * per + k], 0, 0, 0))
                for k in range(per)
            ]
            + [pl.BlockSpec((block, 2 * rank), lambda b, t: (skip + b, 0)) for _ in low_parts]
            + specs
            + [HERE] * len(after),
            out_specs=pl.BlockSpec((block, 2 * chunk), lambda b, t: (b, 0)),
        ),
        out_shape=jax.ShapeDtypeStruct((rows, 2 * chunk), jnp.bfloat16),
        compiler_params=params(),
        cost_estimate=estimate(2 * rows / block),
    )(tenants, *[up_maps] * per, *low_parts, *operands, *after)


def finish(start, rows, out_rows, terms, previous):
    chunk = terms[0][0][1].shape[1] // 2
    block = 512 if rows % 512 == start % 512 == 0 else 256
    skip = start // block
    specs, operands, layout = segment_specs(terms, start, block)
    aliases = {}
    if previous is not None:
        aliases = {len(operands): 0}
        specs.append(HERE)
        operands.append(previous)

    def body(*refs):
        total = term_sum(pl.program_id(0), refs, layout)
        refs[-1][...] = total.astype(jnp.bfloat16).reshape(block, 2, chunk)

    return pl.pallas_call(
        body,
        name="finish",
        grid=(rows // block,),
        in_specs=specs,
        out_specs=pl.BlockSpec((block, 2, chunk), lambda i: (skip + i, 0, 0)),
        out_shape=jax.ShapeDtypeStruct((out_rows, 2, chunk), jnp.bfloat16),
        input_output_aliases=aliases,
        compiler_params=params(),
        cost_estimate=estimate(1.3 * rows / block),
    )(*operands)


def local(n, hidden, key_value_weight, adapter_down_weight, adapter_up_weight, tenant_per_block):
    tok_rows, local_width = hidden.shape
    chunk = adapter_up_weight.shape[3]
    unit = tok_rows // UNITS
    slots, sends = line_plan(n)

    down_maps = lax.all_gather(adapter_down_weight, "tok", axis=0, tiled=True)
    up_maps = lax.all_gather(adapter_up_weight, "tok", axis=0, tiled=True)

    place = lax.axis_index("tp").reshape(1)
    which = slots.T
    partial = {}
    received = {}
    last = []

    def pick(segments, start, rows):
        return [(f, a) for f, a in segments if f < start + rows and start < f + a.shape[0]]

    def ordered(array):
        last[:] = [array]
        return array

    def cut(arrays, start=0):
        segments = []
        for array in arrays:
            segments.append((start, array))
            start += array.shape[0]
        return segments

    def send(time, parity, u, count, after=(), again=False):
        start, rows = u * unit, count * unit
        ks = sorted({k for _, _, k in sends[time, parity]})
        earlier = pick(received.get((time - 1, 1 - parity), []), start, rows)
        own = pick(partial[ks[0]], start, rows)
        if len(ks) > 1:
            table = np.zeros((n,), np.int32)
            for i, _, k in sends[time, parity]:
                table[i] = k
            mine = by_device(table, "tp")
            ((_, value),) = own
            for k in ks[1:]:
                ((_, other),) = pick(partial[k], start, rows)
                value = jnp.where(mine == k, other, value)
            own = [(start, value)]
        if earlier or again:
            terms = [own, earlier] if earlier else [own]
            value = ordered(added(start, rows, terms, last + list(after)))
        else:
            ((_, value),) = own
        moves = [(i, to) for i, to, _ in sends[time, parity]]
        with jax.named_scope(f"{'odd' if parity else 'even'}{time}_units{u}"):
            moved = lax.ppermute(value, "tp", moves)
        received.setdefault((time, parity), []).append((start, moved))
        return received[time, parity][-1][1]

    low_parts = []

    def send_low(time, after=()):
        value = low_parts[0]
        if time > 1:
            value = ordered(added(0, tok_rows, [[(0, value)], [(0, low_parts[-1])]], last + list(after)))
        with jax.named_scope(f"low_sums{time}"):
            low_parts.append(lax.ppermute(value, "tp", [(time - 1, time), (n - time, n - time - 1)]))

    ready = []

    def prepare(u, count):
        start, rows = u * unit, count * unit
        terms = [pick(partial[n - 1], start, rows)]
        value = with_adapter(start, rows, terms, low_parts, up_maps, tenant_per_block, list(last))
        ready.append((start, ordered(value)))

    result = [None]

    def complete(u, count):
        start, rows = u * unit, count * unit
        terms = [pick(ready, start, rows)] + [pick(received[n - 1, parity], start, rows) for parity in (0, 1)]
        result[0] = finish(start, rows, tok_rows, terms, result[0])

    first = 2 * unit
    flat, head = first_piece(hidden, key_value_weight, place, which[0], first, chunk)
    partial[0] = [(0, head)]
    if n == 4:
        arrived = send(1, 0, 0, 2)
        partial[0] += cut(more_rows(hidden, flat, first, [first] * 3, []), first)
        for u in (2, 4, 6):
            send(1, 0, u, 2)

        def others(s, cuts, after):
            results = other_slots(
                hidden, key_value_weight, place, which[s : s + len(cuts)], cuts, chunk, after
            )
            for k, arrays in enumerate(results):
                partial[s + k] = cut(arrays)
            ordered(results[0][0])

        others(1, [[tok_rows // 2] * 2], [partial[0][-1][1], arrived])
        send(2, 0, 0, 4)
        send(2, 1, 0, 4)
        others(2, [[tok_rows], [tok_rows]], list(last))
        send(2, 1, 4, 4)
        low_parts.append(ordered(low_terms(hidden, down_maps, tenant_per_block, list(last))))
        send_low(1)
        send(2, 0, 4, 4, again=True)
        send(3, 1, 0, 4)
        send(3, 0, 0, 4)
        send_low(2)
        send(3, 0, 4, 2)
        send_low(3)
        send(3, 1, 4, 4)
        send(3, 0, 6, 2)
        prepare(0, 8)
        complete(0, 4)
        complete(4, 2)
        complete(6, 2)
    else:
        partial[0] = [
            (0, jnp.concatenate([head] + list(more_rows(hidden, flat, first, [tok_rows - first], []))))
        ]
        others = other_slots(hidden, key_value_weight, place, which[1:], [[tok_rows]] * (n - 1), chunk, [head])
        for s, arrays in enumerate(others):
            partial[s + 1] = cut(arrays)
        ordered(head)
        for time in range(1, n):
            for parity in (0, 1):
                if (time, parity) in sends:
                    send(time, parity, 0, UNITS)
        low_parts.append(ordered(low_terms(hidden, down_maps, tenant_per_block, list(last))))
        for time in range(1, n):
            send_low(time)
        prepare(0, UNITS)
        complete(0, UNITS)
    return result[0]


def solution(mesh):
    n = mesh.shape["tp"]
    in_specs = (
        P("tok", "tp"),
        P("tp", None, None),
        P("tok", "tp", None),
        P("tok", None, None, "tp"),
        P("tok"),
    )
    out_specs = P("tok", None, "tp")

    def run(*args):
        return local(n, *args)

    return jax.shard_map(run, mesh=mesh, in_specs=in_specs, out_specs=out_specs, check_vma=False)
```

```python
import jax
import jax.numpy as jnp
import numpy as np
from jax import lax
from jax.experimental import pallas as pl
from jax.experimental.pallas import tpu as pltpu
from jax.sharding import PartitionSpec as P

UNITS = 8
SCALE = 0.25
VMEM_BYTES = 64 * 1024 * 1024 - 256 * 1024


def line_plan(n):
    sends = {}
    slots = np.zeros((n, n), np.int32)
    for i in range(n):
        order = []
        for c in range(n):
            if c == i:
                continue
            forward = c > i
            time = n - c + i if forward else c + n - i
            parity = (i if forward else i - 1) % 2
            order.append((time, 1 - parity, c, parity, i + 1 if forward else i - 1))
        order.sort()
        for k, (time, _, c, parity, to) in enumerate(order):
            slots[i, k] = c
            sends.setdefault((time, parity), []).append((i, to, k))
        slots[i, n - 1] = i
    return slots, sends


def by_device(table, axis):
    return jnp.asarray(table)[lax.axis_index(axis)]


def chunk_of(table, place):
    value = int(table[0])
    for i in range(1, len(table)):
        value = jnp.where(place == i, int(table[i]), value)
    return value


def params():
    return pltpu.CompilerParams(vmem_limit_bytes=VMEM_BYTES)


def estimate(microseconds):
    return pl.CostEstimate(flops=1, bytes_accessed=int(microseconds * 3.69e6 * SCALE), transcendentals=0)


HERE = pl.BlockSpec(memory_space=pl.ANY)


def first_piece(hidden, weight, place, which, rows, chunk, after):
    width = hidden.shape[1]
    steps = 2
    depth = width // steps

    def body(place_ref, hidden_ref, weight_ref, *refs):
        flat_ref, out_ref, total = refs[-3:]
        k = pl.program_id(0)
        flat_ref[...] = weight_ref[...].reshape(depth, 2 * chunk)
        term = jnp.dot(hidden_ref[...], flat_ref[...], preferred_element_type=jnp.float32)

        @pl.when(k == 0)
        def _():
            total[...] = term

        @pl.when(k > 0)
        def _():
            total[...] += term

        @pl.when(k == steps - 1)
        def _():
            out_ref[...] = total[...].astype(out_ref.dtype)

    return pl.pallas_call(
        body,
        name="first_piece",
        grid_spec=pltpu.PrefetchScalarGridSpec(
            num_scalar_prefetch=1,
            grid=(steps,),
            in_specs=[
                pl.BlockSpec((rows, depth), lambda k, c: (0, k)),
                pl.BlockSpec((depth, 2, chunk), lambda k, c: (k, 0, chunk_of(which, c[0]))),
            ]
            + [HERE] * len(after),
            out_specs=[
                pl.BlockSpec((depth, 2 * chunk), lambda k, c: (k, 0)),
                pl.BlockSpec((rows, 2 * chunk), lambda k, c: (0, 0)),
            ],
            scratch_shapes=[pltpu.VMEM((rows, 2 * chunk), jnp.float32)],
        ),
        out_shape=[
            jax.ShapeDtypeStruct((width, 2 * chunk), jnp.bfloat16),
            jax.ShapeDtypeStruct((rows, 2 * chunk), jnp.bfloat16),
        ],
        compiler_params=params(),
        cost_estimate=estimate(5.5),
    )(place, hidden, weight, *after)


def row_outputs(cuts, block, columns):
    specs, shapes, places = [], [], []
    first = 0
    for rows in cuts:
        count = rows // block

        def index(i, first=first, count=count):
            return jnp.clip(i - first, 0, count - 1), 0

        specs.append((block, columns, index))
        shapes.append(jax.ShapeDtypeStruct((rows, columns), jnp.bfloat16))
        places.append((first, first + count))
        first += count
    return specs, shapes, places


def more_rows(hidden, flat, start, cuts, after):
    width, columns = flat.shape
    block = 512
    skip = start // block
    specs, shapes, places = row_outputs(cuts, block, columns)

    def body(hidden_ref, flat_ref, *refs):
        i = pl.program_id(0)
        value = jnp.dot(hidden_ref[...], flat_ref[...], preferred_element_type=jnp.float32).astype(jnp.bfloat16)
        for ref, (low, high) in zip(refs[len(after) :], places):

            @pl.when((i >= low) & (i < high))
            def _(ref=ref):
                ref[...] = value

    return pl.pallas_call(
        body,
        name="more_rows",
        grid=(sum(cuts) // block,),
        in_specs=[
            pl.BlockSpec((block, width), lambda i: (skip + i, 0)),
            pl.BlockSpec((width, columns), lambda i: (0, 0)),
        ]
        + [HERE] * len(after),
        out_specs=[pl.BlockSpec((b, c), index) for b, c, index in specs],
        out_shape=shapes,
        compiler_params=params(),
        cost_estimate=estimate(2.5 * sum(cuts) / block),
    )(hidden, flat, *after)


def other_slots(hidden, weight, place, which, cuts, chunk, after):
    tok_rows, width = hidden.shape
    count = len(cuts)
    steps = 4
    depth = width // steps
    block = 512
    out_specs, out_shapes, targets = [], [], []
    for slot_cuts in cuts:
        specs, shapes, places = row_outputs(slot_cuts, block, 2 * chunk)
        targets.append([(len(out_specs) + k, place) for k, place in enumerate(places)])
        for b, c, index in specs:
            out_specs.append(pl.BlockSpec((b, c), lambda i, w, index=index: index(i - steps)))
        out_shapes += shapes

    def body(which_ref, hidden_ref, *refs):
        weight_refs = refs[:count]
        outs = refs[count + len(after) : -1]
        flat = refs[-1]
        i = pl.program_id(0)

        @pl.when(i < steps)
        def _():
            for s in range(count):
                flat[s, pl.ds(pl.multiple_of(i * depth, depth), depth), :] = weight_refs[s][...].reshape(
                    depth, 2 * chunk
                )

        @pl.when(i >= steps)
        def _():
            for s in range(count):
                value = jnp.dot(hidden_ref[...], flat[s], preferred_element_type=jnp.float32).astype(jnp.bfloat16)
                for k, (low, high) in targets[s]:

                    @pl.when((i >= steps + low) & (i < steps + high))
                    def _(k=k, value=value):
                        outs[k][...] = value

    arrays = pl.pallas_call(
        body,
        name="other_slots",
        grid_spec=pltpu.PrefetchScalarGridSpec(
            num_scalar_prefetch=1,
            grid=(steps + tok_rows // block,),
            in_specs=[pl.BlockSpec((block, width), lambda i, w: (jnp.maximum(i - steps, 0), 0))]
            + [
                pl.BlockSpec((depth, 2, chunk), lambda i, w, s=s: (jnp.minimum(i, steps - 1), 0, chunk_of(which[s], w[0])))
                for s in range(count)
            ]
            + [HERE] * len(after),
            out_specs=out_specs,
            scratch_shapes=[pltpu.VMEM((count, width, 2 * chunk), jnp.bfloat16)],
        ),
        out_shape=out_shapes,
        compiler_params=params(),
        cost_estimate=estimate(8 + 1.3 * count * tok_rows / block),
    )(place, hidden, *[weight] * count, *after)
    return [[arrays[k] for k, _ in target] for target in targets]


def segment_specs(terms, start, block):
    specs, operands, layout = [], [], []
    for term in terms:
        places = []
        for first, array in term:
            count = array.shape[0] // block
            places.append((len(operands), (first - start) // block))
            operands.append(array)

            def index(i, *_, shift=(first - start) // block, count=count):
                return jnp.clip(i - shift, 0, count - 1), 0

            specs.append(pl.BlockSpec((block, array.shape[1]), index))
        layout.append(places)
    return specs, operands, layout


def term_sum(i, refs, layout):
    total = None
    for places in layout:
        value = refs[places[0][0]][...].astype(jnp.float32)
        for place, shift in places[1:]:
            value = jnp.where(i >= shift, refs[place][...].astype(jnp.float32), value)
        total = value if total is None else total + value
    return total


def added(start, rows, terms, after):
    columns = terms[0][0][1].shape[1]
    block = rows if columns <= 128 else 512 if rows % 512 == start % 512 == 0 else 256
    specs, operands, layout = segment_specs(terms, start, block)

    def body(*refs):
        refs[-1][...] = term_sum(pl.program_id(0), refs, layout).astype(jnp.bfloat16)

    return pl.pallas_call(
        body,
        name="added",
        grid=(rows // block,),
        in_specs=specs + [HERE] * len(after),
        out_specs=pl.BlockSpec((block, columns), lambda i: (i, 0)),
        out_shape=jax.ShapeDtypeStruct((rows, columns), jnp.bfloat16),
        compiler_params=params(),
        cost_estimate=estimate(1.3 * rows * columns / 262144),
    )(*operands, *after)


def copied(arrays, after):
    count, rows, columns = arrays[0].shape

    def body(*refs):
        for k in range(len(arrays)):
            refs[k - len(arrays)][...] = refs[k][...]

    block = pl.BlockSpec((1, rows, columns), lambda i: (i, 0, 0))
    return pl.pallas_call(
        body,
        name="copied",
        grid=(count,),
        in_specs=[block] * len(arrays) + [HERE] * len(after),
        out_specs=[block] * len(arrays),
        out_shape=[jax.ShapeDtypeStruct(array.shape, array.dtype) for array in arrays],
        compiler_params=params(),
        cost_estimate=estimate(2),
    )(*arrays, *after)


def low_terms(hidden, sources, places, after):
    tok_rows, width = hidden.shape
    count = places.shape[0]
    rows = tok_rows // count
    length, _, columns = sources[0].shape
    per = 4

    def body(place_ref, hidden_ref, *refs):
        source_refs = refs[: len(sources)]
        out_ref, maps, sems = refs[-3:]
        i = pl.program_id(0)

        def fetch(source, index, b):
            return pltpu.make_async_copy(source.at[index, pl.ds(0, width)], maps.at[b], sems.at[b])

        @pl.when(i == 0)
        def _():
            for b in range(count):
                place = place_ref[b]
                for k, source in enumerate(source_refs):

                    @pl.when(place // length == k)
                    def _(source=source, place=place, b=b, k=k):
                        fetch(source, place - k * length, b).start()

        for k in range(per):
            b = i * per + k
            fetch(source_refs[0], 0, b).wait()
            part = slice(k * rows, (k + 1) * rows)
            out_ref[part, :] = jnp.dot(
                hidden_ref[part, :], maps[b], preferred_element_type=jnp.float32
            ).astype(jnp.bfloat16)

    return pl.pallas_call(
        body,
        name="low_terms",
        grid_spec=pltpu.PrefetchScalarGridSpec(
            num_scalar_prefetch=1,
            grid=(count // per,),
            in_specs=[pl.BlockSpec((per * rows, width), lambda b, t: (b, 0))]
            + [HERE] * (len(sources) + len(after)),
            out_specs=pl.BlockSpec((per * rows, columns), lambda b, t: (b, 0)),
            scratch_shapes=[
                pltpu.VMEM((count, width, columns), jnp.bfloat16),
                pltpu.SemaphoreType.DMA((count,)),
            ],
        ),
        out_shape=jax.ShapeDtypeStruct((tok_rows, columns), jnp.bfloat16),
        compiler_params=params(),
        cost_estimate=estimate(8.6),
    )(places, hidden, *sources, *after)


def finish(start, rows, block, out_rows, terms, low_parts, up_maps, tenants, previous, after):
    rank, chunk = up_maps.shape[2:]
    blk_rows = low_parts[0].shape[0] // tenants.shape[0]
    per = block // blk_rows
    skip = start // block
    specs, operands, layout = segment_specs(terms, start, block)
    n_low = len(low_parts)
    kept = [] if previous is None else [previous]

    def body(tenant_ref, *refs):
        up_refs, low_refs, term_refs = refs[:per], refs[per : per + n_low], refs[per + n_low :]
        out_ref = refs[-1]
        low = low_refs[0][...].astype(jnp.float32)
        for ref in low_refs[1:]:
            low = low + ref[...].astype(jnp.float32)
        low = low.astype(jnp.bfloat16)
        total = term_sum(pl.program_id(0), term_refs, layout)
        for k in range(per):
            part = slice(k * blk_rows, (k + 1) * blk_rows)
            adapt = jnp.concatenate(
                [
                    jnp.dot(
                        low[part, h * rank : (h + 1) * rank], up_refs[k][0, h], preferred_element_type=jnp.float32
                    )
                    for h in range(2)
                ],
                axis=1,
            )
            out_ref[part] = (total[part] + adapt).astype(jnp.bfloat16).reshape(blk_rows, 2, chunk)

    operands = [up_maps] * per + list(low_parts) + operands + list(after) + kept
    return pl.pallas_call(
        body,
        name="finish",
        grid_spec=pltpu.PrefetchScalarGridSpec(
            num_scalar_prefetch=1,
            grid=(rows // block,),
            in_specs=[
                pl.BlockSpec((1, 2, rank, chunk), lambda b, t, k=k: (t[(skip + b) * per + k], 0, 0, 0))
                for k in range(per)
            ]
            + [pl.BlockSpec((block, 2 * rank), lambda b, t: (skip + b, 0)) for _ in low_parts]
            + specs
            + [HERE] * (len(after) + len(kept)),
            out_specs=pl.BlockSpec((block, 2, chunk), lambda b, t: (skip + b, 0, 0)),
        ),
        out_shape=jax.ShapeDtypeStruct((out_rows, 2, chunk), jnp.bfloat16),
        input_output_aliases={len(operands): 0} if kept else {},
        compiler_params=params(),
        cost_estimate=estimate(2 * rows / block),
    )(tenants, *operands)


def local(n, n_tok, hidden, key_value_weight, adapter_down_weight, adapter_up_weight, tenant_per_block):
    tok_rows, local_width = hidden.shape
    chunk = adapter_up_weight.shape[3]
    unit = tok_rows // UNITS
    slots, sends = line_plan(n)

    place = lax.axis_index("tp").reshape(1)
    which = slots.T
    partial = {}
    received = {}
    last = []

    def pick(segments, start, rows):
        return [(f, a) for f, a in segments if f < start + rows and start < f + a.shape[0]]

    def ordered(array):
        last[:] = [array]
        return array

    def cut(arrays, start=0):
        segments = []
        for array in arrays:
            segments.append((start, array))
            start += array.shape[0]
        return segments

    def send(time, parity, u, count, after=(), again=False):
        start, rows = u * unit, count * unit
        ks = sorted({k for _, _, k in sends[time, parity]})
        earlier = pick(received.get((time - 1, 1 - parity), []), start, rows)
        own = pick(partial[ks[0]], start, rows)
        if len(ks) > 1:
            table = np.zeros((n,), np.int32)
            for i, _, k in sends[time, parity]:
                table[i] = k
            mine = by_device(table, "tp")
            ((_, value),) = own
            for k in ks[1:]:
                ((_, other),) = pick(partial[k], start, rows)
                value = jnp.where(mine == k, other, value)
            own = [(start, value)]
        if earlier or again:
            terms = [own, earlier] if earlier else [own]
            value = ordered(added(start, rows, terms, last + list(after)))
        else:
            ((_, value),) = own
        moves = [(i, to) for i, to, _ in sends[time, parity]]
        with jax.named_scope(f"{'odd' if parity else 'even'}{time}_units{u}"):
            moved = lax.ppermute(value, "tp", moves)
        received.setdefault((time, parity), []).append((start, moved))
        return received[time, parity][-1][1]

    low_parts = []

    def send_low(time, after=()):
        value = low_parts[0]
        if time > 1:
            value = ordered(added(0, tok_rows, [[(0, value)], [(0, low_parts[-1])]], last + list(after)))
        with jax.named_scope(f"low_sums{time}"):
            low_parts.append(lax.ppermute(value, "tp", [(time - 1, time), (n - time, n - time - 1)]))

    result = [None]

    def complete(u, count, block, after=()):
        start, rows = u * unit, count * unit
        terms = [pick(partial[n - 1], start, rows)]
        terms += [pick(received[n - 1, parity], start, rows) for parity in (0, 1)]
        result[0] = finish(
            start, rows, block, tok_rows, terms, low_parts, up_maps, tenant_per_block, result[0], after
        )

    first = 4 * unit
    held = adapter_down_weight.shape[0]
    maps = adapter_down_weight
    flat, head = first_piece(hidden, key_value_weight, place, which[0], first, chunk, [])
    partial[0] = [(0, ordered(head))]

    def others(s, cuts, after):
        results = other_slots(hidden, key_value_weight, place, which[s : s + len(cuts)], cuts, chunk, after)
        for k, arrays in enumerate(results):
            partial[s + k] = cut(arrays)
        ordered(results[0][0])

    if n == 4 and n_tok == 8:
        def fetch(name, array, bits):
            with jax.named_scope(name):
                return lax.ppermute(array, "tok", [(i, i ^ bits) for i in range(n_tok)])

        places = ((tenant_per_block // held) ^ lax.axis_index("tok")) * held + tenant_per_block % held
        other_core, other_x, other_y = [fetch(f"maps_{bits}", maps, bits) for bits in (1, 2, 4)]
        send(1, 0, 0, 4)
        partial[0] += cut(more_rows(hidden, flat, first, [first], list(last)), first)
        ordered(partial[0][1][1])
        send(1, 0, 4, 4)
        (again,) = copied([maps], last + [other_core, other_x, other_y])
        ordered(again)
        x_core, y_core = [fetch(f"maps_{bits}", again, bits) for bits in (3, 5)]
        others(1, [[tok_rows // 2] * 2], list(last))
        send(2, 0, 0, 4)
        upper = send(2, 1, 0, 4)
        others(2, [[tok_rows]], list(last))
        lower = send(2, 1, 4, 4)
        x_again, y_again = copied([x_core, y_core], list(last))
        ordered(x_again)
        sources = [maps, other_core, other_x, x_core, other_y, y_core]
        sources += [fetch("maps_6", x_again, 5), fetch("maps_7", y_again, 2)]
        second = send(2, 0, 4, 4, after=[upper], again=True)
        others(3, [[tok_rows]], list(last))
        third = send(3, 1, 0, 4)
        low_parts.append(ordered(low_terms(hidden, sources, places, list(last))))
        send_low(1)
        fourth = send(3, 0, 0, 4, after=[lower, second])
        with jax.named_scope("up_maps"):
            ups = jnp.broadcast_to(adapter_up_weight, (n_tok,) + adapter_up_weight.shape)
            ups = lax.all_to_all(ups, "tok", 0, 0, tiled=True)
        up_maps = ups.reshape((n_tok * held,) + adapter_up_weight.shape[1:])
        send_low(2, after=[third])
        send(3, 1, 4, 4)
        fifth = send(3, 0, 4, 2)
        send_low(3, after=[up_maps])
        send(3, 0, 6, 2, after=[fourth])
        complete(0, 4, 512, after=[fifth])
        complete(4, 2, 512)
        complete(6, 2, 256)
    else:
        places = tenant_per_block
        sources = [lax.all_gather(maps, "tok", axis=0, tiled=True)]
        up_maps = lax.all_gather(adapter_up_weight, "tok", axis=0, tiled=True)
        lower = more_rows(hidden, flat, first, [tok_rows - first], list(last))[0]
        partial[0] = [(0, jnp.concatenate([head, lower]))]
        others(1, [[tok_rows]] * (n - 1), list(last))
        for time in range(1, n):
            for parity in (0, 1):
                if (time, parity) in sends:
                    send(time, parity, 0, UNITS)
        low_parts.append(ordered(low_terms(hidden, sources, places, list(last))))
        for time in range(1, n):
            send_low(time)
        complete(0, UNITS, 512)
    return result[0]


def solution(mesh):
    n, n_tok = mesh.shape["tp"], mesh.shape["tok"]
    in_specs = (
        P("tok", "tp"),
        P("tp", None, None),
        P("tok", "tp", None),
        P("tok", None, None, "tp"),
        P("tok"),
    )
    out_specs = P("tok", None, "tp")

    def run(*args):
        return local(n, n_tok, *args)

    return jax.shard_map(run, mesh=mesh, in_specs=in_specs, out_specs=out_specs, check_vma=False)
```

```python
import jax
import jax.numpy as jnp
import numpy as np
from jax import lax
from jax.experimental import pallas as pl
from jax.experimental.pallas import tpu as pltpu
from jax.sharding import PartitionSpec as P

UNITS = 8
SCALE = 0.25
VMEM_BYTES = 64 * 1024 * 1024 - 256 * 1024


def line_plan(n):
    sends = {}
    slots = np.zeros((n, n), np.int32)
    for i in range(n):
        order = []
        for c in range(n):
            if c == i:
                continue
            forward = c > i
            time = n - c + i if forward else c + n - i
            parity = (i if forward else i - 1) % 2
            order.append((time, 1 - parity, c, parity, i + 1 if forward else i - 1))
        order.sort()
        for k, (time, _, c, parity, to) in enumerate(order):
            slots[i, k] = c
            sends.setdefault((time, parity), []).append((i, to, k))
        slots[i, n - 1] = i
    return slots, sends


def by_device(table, axis):
    return jnp.asarray(table)[lax.axis_index(axis)]


def chunk_of(table, place):
    value = int(table[0])
    for i in range(1, len(table)):
        value = jnp.where(place == i, int(table[i]), value)
    return value


def params():
    return pltpu.CompilerParams(vmem_limit_bytes=VMEM_BYTES)


def estimate(microseconds):
    return pl.CostEstimate(flops=1, bytes_accessed=int(microseconds * 3.69e6 * SCALE), transcendentals=0)


HERE = pl.BlockSpec(memory_space=pl.ANY)


def first_piece(hidden, weight, place, which, rows, chunk, after):
    width = hidden.shape[1]
    steps = 2
    depth = width // steps

    def body(place_ref, hidden_ref, weight_ref, *refs):
        flat_ref, out_ref, total = refs[-3:]
        k = pl.program_id(0)
        flat_ref[...] = weight_ref[...].reshape(depth, 2 * chunk)
        term = jnp.dot(hidden_ref[...], flat_ref[...], preferred_element_type=jnp.float32)

        @pl.when(k == 0)
        def _():
            total[...] = term

        @pl.when(k > 0)
        def _():
            total[...] += term

        @pl.when(k == steps - 1)
        def _():
            out_ref[...] = total[...].astype(out_ref.dtype)

    return pl.pallas_call(
        body,
        name="first_piece",
        grid_spec=pltpu.PrefetchScalarGridSpec(
            num_scalar_prefetch=1,
            grid=(steps,),
            in_specs=[
                pl.BlockSpec((rows, depth), lambda k, c: (0, k)),
                pl.BlockSpec((depth, 2, chunk), lambda k, c: (k, 0, chunk_of(which, c[0]))),
            ]
            + [HERE] * len(after),
            out_specs=[
                pl.BlockSpec((depth, 2 * chunk), lambda k, c: (k, 0)),
                pl.BlockSpec((rows, 2 * chunk), lambda k, c: (0, 0)),
            ],
            scratch_shapes=[pltpu.VMEM((rows, 2 * chunk), jnp.float32)],
        ),
        out_shape=[
            jax.ShapeDtypeStruct((width, 2 * chunk), jnp.bfloat16),
            jax.ShapeDtypeStruct((rows, 2 * chunk), jnp.bfloat16),
        ],
        compiler_params=params(),
        cost_estimate=estimate(5.5),
    )(place, hidden, weight, *after)


def row_outputs(cuts, block, columns):
    specs, shapes, places = [], [], []
    first = 0
    for rows in cuts:
        count = rows // block

        def index(i, first=first, count=count):
            return jnp.clip(i - first, 0, count - 1), 0

        specs.append((block, columns, index))
        shapes.append(jax.ShapeDtypeStruct((rows, columns), jnp.bfloat16))
        places.append((first, first + count))
        first += count
    return specs, shapes, places


def more_rows(hidden, flat, start, cuts, after):
    width, columns = flat.shape
    block = 512
    skip = start // block
    specs, shapes, places = row_outputs(cuts, block, columns)

    def body(hidden_ref, flat_ref, *refs):
        i = pl.program_id(0)
        value = jnp.dot(hidden_ref[...], flat_ref[...], preferred_element_type=jnp.float32).astype(jnp.bfloat16)
        for ref, (low, high) in zip(refs[len(after) :], places):

            @pl.when((i >= low) & (i < high))
            def _(ref=ref):
                ref[...] = value

    return pl.pallas_call(
        body,
        name="more_rows",
        grid=(sum(cuts) // block,),
        in_specs=[
            pl.BlockSpec((block, width), lambda i: (skip + i, 0)),
            pl.BlockSpec((width, columns), lambda i: (0, 0)),
        ]
        + [HERE] * len(after),
        out_specs=[pl.BlockSpec((b, c), index) for b, c, index in specs],
        out_shape=shapes,
        compiler_params=params(),
        cost_estimate=estimate(2.5 * sum(cuts) / block),
    )(hidden, flat, *after)


def other_slots(hidden, weight, place, which, cuts, chunk, after):
    tok_rows, width = hidden.shape
    count = len(cuts)
    steps = 4
    depth = width // steps
    block = 512
    out_specs, out_shapes, targets = [], [], []
    for slot_cuts in cuts:
        specs, shapes, places = row_outputs(slot_cuts, block, 2 * chunk)
        targets.append([(len(out_specs) + k, place) for k, place in enumerate(places)])
        for b, c, index in specs:
            out_specs.append(pl.BlockSpec((b, c), lambda i, w, index=index: index(i - steps)))
        out_shapes += shapes

    def body(which_ref, hidden_ref, *refs):
        weight_refs = refs[:count]
        outs = refs[count + len(after) : -1]
        flat = refs[-1]
        i = pl.program_id(0)

        @pl.when(i < steps)
        def _():
            for s in range(count):
                flat[s, pl.ds(pl.multiple_of(i * depth, depth), depth), :] = weight_refs[s][...].reshape(
                    depth, 2 * chunk
                )

        @pl.when(i >= steps)
        def _():
            for s in range(count):
                value = jnp.dot(hidden_ref[...], flat[s], preferred_element_type=jnp.float32).astype(jnp.bfloat16)
                for k, (low, high) in targets[s]:

                    @pl.when((i >= steps + low) & (i < steps + high))
                    def _(k=k, value=value):
                        outs[k][...] = value

    arrays = pl.pallas_call(
        body,
        name="other_slots",
        grid_spec=pltpu.PrefetchScalarGridSpec(
            num_scalar_prefetch=1,
            grid=(steps + tok_rows // block,),
            in_specs=[pl.BlockSpec((block, width), lambda i, w: (jnp.maximum(i - steps, 0), 0))]
            + [
                pl.BlockSpec((depth, 2, chunk), lambda i, w, s=s: (jnp.minimum(i, steps - 1), 0, chunk_of(which[s], w[0])))
                for s in range(count)
            ]
            + [HERE] * len(after),
            out_specs=out_specs,
            scratch_shapes=[pltpu.VMEM((count, width, 2 * chunk), jnp.bfloat16)],
        ),
        out_shape=out_shapes,
        compiler_params=params(),
        cost_estimate=estimate(8 + 1.3 * count * tok_rows / block),
    )(place, hidden, *[weight] * count, *after)
    return [[arrays[k] for k, _ in target] for target in targets]


def segment_specs(terms, start, block):
    specs, operands, layout = [], [], []
    for term in terms:
        places = []
        for first, array in term:
            count = array.shape[0] // block
            places.append((len(operands), (first - start) // block))
            operands.append(array)

            def index(i, *_, shift=(first - start) // block, count=count):
                return jnp.clip(i - shift, 0, count - 1), 0

            specs.append(pl.BlockSpec((block, array.shape[1]), index))
        layout.append(places)
    return specs, operands, layout


def term_sum(i, refs, layout):
    total = None
    for places in layout:
        value = refs[places[0][0]][...].astype(jnp.float32)
        for place, shift in places[1:]:
            value = jnp.where(i >= shift, refs[place][...].astype(jnp.float32), value)
        total = value if total is None else total + value
    return total


def added(start, rows, terms, after):
    columns = terms[0][0][1].shape[1]
    block = rows if columns <= 128 else 512 if rows % 512 == start % 512 == 0 else 256
    specs, operands, layout = segment_specs(terms, start, block)

    def body(*refs):
        refs[-1][...] = term_sum(pl.program_id(0), refs, layout).astype(jnp.bfloat16)

    return pl.pallas_call(
        body,
        name="added",
        grid=(rows // block,),
        in_specs=specs + [HERE] * len(after),
        out_specs=pl.BlockSpec((block, columns), lambda i: (i, 0)),
        out_shape=jax.ShapeDtypeStruct((rows, columns), jnp.bfloat16),
        compiler_params=params(),
        cost_estimate=estimate(1.3 * rows * columns / 262144),
    )(*operands, *after)


def copied(arrays, after):
    count, rows, columns = arrays[0].shape

    def body(*refs):
        for k in range(len(arrays)):
            refs[k - len(arrays)][...] = refs[k][...]

    block = pl.BlockSpec((1, rows, columns), lambda i: (i, 0, 0))
    return pl.pallas_call(
        body,
        name="copied",
        grid=(count,),
        in_specs=[block] * len(arrays) + [HERE] * len(after),
        out_specs=[block] * len(arrays),
        out_shape=[jax.ShapeDtypeStruct(array.shape, array.dtype) for array in arrays],
        compiler_params=params(),
        cost_estimate=estimate(2),
    )(*arrays, *after)


def low_terms(hidden, sources, places, after):
    tok_rows, width = hidden.shape
    count = places.shape[0]
    rows = tok_rows // count
    length, _, columns = sources[0].shape
    per = 4

    def body(place_ref, hidden_ref, *refs):
        source_refs = refs[: len(sources)]
        out_ref, maps, sems = refs[-3:]
        i = pl.program_id(0)

        def fetch(source, index, b):
            return pltpu.make_async_copy(source.at[index, pl.ds(0, width)], maps.at[b], sems.at[b])

        @pl.when(i == 0)
        def _():
            for b in range(count):
                place = place_ref[b]
                for k, source in enumerate(source_refs):

                    @pl.when(place // length == k)
                    def _(source=source, place=place, b=b, k=k):
                        fetch(source, place - k * length, b).start()

        for k in range(per):
            b = i * per + k
            fetch(source_refs[0], 0, b).wait()
            part = slice(k * rows, (k + 1) * rows)
            out_ref[part, :] = jnp.dot(
                hidden_ref[part, :], maps[b], preferred_element_type=jnp.float32
            ).astype(jnp.bfloat16)

    return pl.pallas_call(
        body,
        name="low_terms",
        grid_spec=pltpu.PrefetchScalarGridSpec(
            num_scalar_prefetch=1,
            grid=(count // per,),
            in_specs=[pl.BlockSpec((per * rows, width), lambda b, t: (b, 0))]
            + [HERE] * (len(sources) + len(after)),
            out_specs=pl.BlockSpec((per * rows, columns), lambda b, t: (b, 0)),
            scratch_shapes=[
                pltpu.VMEM((count, width, columns), jnp.bfloat16),
                pltpu.SemaphoreType.DMA((count,)),
            ],
        ),
        out_shape=jax.ShapeDtypeStruct((tok_rows, columns), jnp.bfloat16),
        compiler_params=params(),
        cost_estimate=estimate(8.6),
    )(places, hidden, *sources, *after)


def finish(start, rows, block, out_rows, terms, low_parts, up_maps, tenants, previous, after):
    rank, chunk = up_maps.shape[2:]
    blk_rows = low_parts[0].shape[0] // tenants.shape[0]
    per = block // blk_rows
    skip = start // block
    specs, operands, layout = segment_specs(terms, start, block)
    n_low = len(low_parts)
    kept = [] if previous is None else [previous]

    def body(tenant_ref, *refs):
        up_refs, low_refs, term_refs = refs[:per], refs[per : per + n_low], refs[per + n_low :]
        out_ref = refs[-1]
        low = low_refs[0][...].astype(jnp.float32)
        for ref in low_refs[1:]:
            low = low + ref[...].astype(jnp.float32)
        low = low.astype(jnp.bfloat16)
        total = term_sum(pl.program_id(0), term_refs, layout)
        for k in range(per):
            part = slice(k * blk_rows, (k + 1) * blk_rows)
            adapt = jnp.concatenate(
                [
                    jnp.dot(
                        low[part, h * rank : (h + 1) * rank], up_refs[k][0, h], preferred_element_type=jnp.float32
                    )
                    for h in range(2)
                ],
                axis=1,
            )
            out_ref[part] = (total[part] + adapt).astype(jnp.bfloat16).reshape(blk_rows, 2, chunk)

    operands = [up_maps] * per + list(low_parts) + operands + list(after) + kept
    return pl.pallas_call(
        body,
        name="finish",
        grid_spec=pltpu.PrefetchScalarGridSpec(
            num_scalar_prefetch=1,
            grid=(rows // block,),
            in_specs=[
                pl.BlockSpec((1, 2, rank, chunk), lambda b, t, k=k: (t[(skip + b) * per + k], 0, 0, 0))
                for k in range(per)
            ]
            + [pl.BlockSpec((block, 2 * rank), lambda b, t: (skip + b, 0)) for _ in low_parts]
            + specs
            + [HERE] * (len(after) + len(kept)),
            out_specs=pl.BlockSpec((block, 2, chunk), lambda b, t: (skip + b, 0, 0)),
        ),
        out_shape=jax.ShapeDtypeStruct((out_rows, 2, chunk), jnp.bfloat16),
        input_output_aliases={len(operands): 0} if kept else {},
        compiler_params=params(),
        cost_estimate=estimate(2 * rows / block),
    )(tenants, *operands)


def local(n, n_tok, hidden, key_value_weight, adapter_down_weight, adapter_up_weight, tenant_per_block):
    tok_rows, local_width = hidden.shape
    chunk = adapter_up_weight.shape[3]
    unit = tok_rows // UNITS
    slots, sends = line_plan(n)

    place = lax.axis_index("tp").reshape(1)
    which = slots.T
    partial = {}
    received = {}
    last = []

    def pick(segments, start, rows):
        return [(f, a) for f, a in segments if f < start + rows and start < f + a.shape[0]]

    def ordered(array):
        last[:] = [array]
        return array

    def cut(arrays, start=0):
        segments = []
        for array in arrays:
            segments.append((start, array))
            start += array.shape[0]
        return segments

    def send(time, parity, u, count, after=(), again=False):
        start, rows = u * unit, count * unit
        ks = sorted({k for _, _, k in sends[time, parity]})
        earlier = pick(received.get((time - 1, 1 - parity), []), start, rows)
        own = pick(partial[ks[0]], start, rows)
        if len(ks) > 1:
            table = np.zeros((n,), np.int32)
            for i, _, k in sends[time, parity]:
                table[i] = k
            mine = by_device(table, "tp")
            ((_, value),) = own
            for k in ks[1:]:
                ((_, other),) = pick(partial[k], start, rows)
                value = jnp.where(mine == k, other, value)
            own = [(start, value)]
        if earlier or again:
            terms = [own, earlier] if earlier else [own]
            value = ordered(added(start, rows, terms, last + list(after)))
        else:
            ((_, value),) = own
        moves = [(i, to) for i, to, _ in sends[time, parity]]
        with jax.named_scope(f"{'odd' if parity else 'even'}{time}_units{u}"):
            moved = lax.ppermute(value, "tp", moves)
        received.setdefault((time, parity), []).append((start, moved))
        return received[time, parity][-1][1]

    low_parts = []

    def send_low(time, after=()):
        value = low_parts[0]
        if time > 1:
            value = ordered(added(0, tok_rows, [[(0, value)], [(0, low_parts[-1])]], last + list(after)))
        with jax.named_scope(f"low_sums{time}"):
            low_parts.append(lax.ppermute(value, "tp", [(time - 1, time), (n - time, n - time - 1)]))

    result = [None]

    def complete(u, count, block, after=()):
        start, rows = u * unit, count * unit
        terms = [pick(partial[n - 1], start, rows)]
        terms += [pick(received[n - 1, parity], start, rows) for parity in (0, 1)]
        result[0] = finish(
            start, rows, block, tok_rows, terms, low_parts, up_maps, tenant_per_block, result[0], after
        )

    first = 4 * unit
    held = adapter_down_weight.shape[0]
    maps = adapter_down_weight
    flat, head = first_piece(hidden, key_value_weight, place, which[0], first, chunk, [])
    partial[0] = [(0, ordered(head))]

    def others(s, cuts, after):
        results = other_slots(hidden, key_value_weight, place, which[s : s + len(cuts)], cuts, chunk, after)
        for k, arrays in enumerate(results):
            partial[s + k] = cut(arrays)
        ordered(results[0][0])

    if n == 4 and n_tok == 8:
        def fetch(name, array, bits):
            with jax.named_scope(name):
                return lax.ppermute(array, "tok", [(i, i ^ bits) for i in range(n_tok)])

        places = ((tenant_per_block // held) ^ lax.axis_index("tok")) * held + tenant_per_block % held
        other_core, other_x, other_y = [fetch(f"maps_{bits}", maps, bits) for bits in (1, 2, 4)]
        send(1, 0, 0, 4)
        partial[0] += cut(more_rows(hidden, flat, first, [first], list(last)), first)
        ordered(partial[0][1][1])
        send(1, 0, 4, 4)
        (again,) = copied([maps], last + [other_core, other_x, other_y])
        ordered(again)
        x_core, y_core = [fetch(f"maps_{bits}", again, bits) for bits in (3, 5)]
        others(1, [[tok_rows // 2] * 2], list(last))
        send(2, 0, 0, 4)
        upper = send(2, 1, 0, 4)
        others(2, [[tok_rows]], list(last))
        lower = send(2, 1, 4, 4)
        x_again, y_again = copied([x_core, y_core], list(last))
        ordered(x_again)
        sources = [maps, other_core, other_x, x_core, other_y, y_core]
        sources += [fetch("maps_6", x_again, 5), fetch("maps_7", y_again, 2)]
        second = send(2, 0, 4, 4, after=[upper], again=True)
        others(3, [[tok_rows]], list(last))
        third = send(3, 1, 0, 4)
        low_parts.append(ordered(low_terms(hidden, sources, places, list(last))))
        send_low(1)
        fourth = send(3, 0, 0, 4, after=[lower, second])
        with jax.named_scope("up_maps"):
            ups = jnp.broadcast_to(adapter_up_weight, (n_tok,) + adapter_up_weight.shape)
            ups = lax.all_to_all(ups, "tok", 0, 0, tiled=True)
        up_maps = ups.reshape((n_tok * held,) + adapter_up_weight.shape[1:])
        fifth = send(3, 0, 4, 2)
        send_low(2, after=[third])
        send(3, 1, 4, 4)
        send_low(3, after=[up_maps])
        send(3, 0, 6, 2, after=[fourth])
        complete(0, 4, 512, after=[fifth])
        complete(4, 2, 512)
        complete(6, 2, 256)
    else:
        places = tenant_per_block
        sources = [lax.all_gather(maps, "tok", axis=0, tiled=True)]
        up_maps = lax.all_gather(adapter_up_weight, "tok", axis=0, tiled=True)
        lower = more_rows(hidden, flat, first, [tok_rows - first], list(last))[0]
        partial[0] = [(0, jnp.concatenate([head, lower]))]
        others(1, [[tok_rows]] * (n - 1), list(last))
        for time in range(1, n):
            for parity in (0, 1):
                if (time, parity) in sends:
                    send(time, parity, 0, UNITS)
        low_parts.append(ordered(low_terms(hidden, sources, places, list(last))))
        for time in range(1, n):
            send_low(time)
        complete(0, UNITS, 512)
    return result[0]


def solution(mesh):
    n, n_tok = mesh.shape["tp"], mesh.shape["tok"]
    in_specs = (
        P("tok", "tp"),
        P("tp", None, None),
        P("tok", "tp", None),
        P("tok", None, None, "tp"),
        P("tok"),
    )
    out_specs = P("tok", None, "tp")

    def run(*args):
        return local(n, n_tok, *args)

    return jax.shard_map(run, mesh=mesh, in_specs=in_specs, out_specs=out_specs, check_vma=False)
```
